32 devices in a mesh: grp: 4 (over y, x), row: 8 (over z, core).
Axes of the slice: x: 2, y: 2, z: 4, core: 2. Of those that a mesh axis runs over, the one named last changes fastest.
Arguments:
- t_start: bfloat16 [8192, 512], P(('row', 'grp')), may hold values from -6 to 6
- h_blocks: bfloat16 [64, 4, 8, 128, 128], P('row', 'grp'), may hold values from -0.09375 to 0.09375
- h_cols: int32 [64, 4, 8], P('row', 'grp'), may hold values from 0 to 63, as said below
- t_cols: int32 [64, 3], P(('row', 'grp')), may hold values from 0 to 3, as said below
Outputs:
- t_before: bfloat16 [8192, 512], P(('row', 'grp'))
- t_last: bfloat16 [8192, 512], P(('row', 'grp'))
The draws below stay inside these ranges and needn't reach their ends.
Inputs may be any that keep to these rules, and one draw needn't show every extreme that they name: The 8 entries of h_cols[b, g] differ, and each names a block row c with (c // 2) % 4 == g. `t_cols`: the 3 entries of a row differ.
All inputs are finite; a program needn't handle non-finite values.
Results may differ from the reference program's by a relative error of at most 0.025.
Values may be sent and summed in bfloat16 or wider, within the bound.
A program may use at most 64 MiB of HBM per device.

```python
import jax
import jax.numpy as jnp
from jax import lax

BS = 128
HB = 32
STEPS = 3
RB = 2
MB = 4
TS = 3
NG = 4
HS = 8
KB = 16
NB = 64
M = 512


def draw_h_cols(key, part):
    scores = jax.random.randint(key, (NB, NG, KB), 0, 1 << 20) * KB + jnp.arange(KB, dtype=jnp.int32)
    order = jnp.argsort(scores, axis=-1)[..., :HS].astype(jnp.int32)
    group = jnp.arange(NG, dtype=jnp.int32)[None, :, None]
    return order // RB * (NG * RB) + group * RB + order % RB


def draw_t_cols(key, part):
    scores = jax.random.randint(key, (NB, MB), 0, 1 << 20) * MB + jnp.arange(MB, dtype=jnp.int32)
    return jnp.argsort(scores, axis=-1)[:, :TS].astype(jnp.int32)


def block_scale(stream_key, dims, cuts, low, largest):
    level = 1.0
    for axis_at, shards_of in cuts:
        steps = jax.random.uniform(jax.random.fold_in(jax.random.fold_in(stream_key, 6), axis_at), (shards_of,), jnp.float32, low / len(cuts), largest / len(cuts))
        level = level * jnp.repeat(jnp.exp(steps), dims[axis_at] // shards_of).reshape((-1,) + (1,) * (len(dims) - 1 - axis_at))
    return level


def scatter_about(rng, dims, deviation, reach, cuts=(), kind=jnp.bfloat16):
    array = deviation * jax.random.normal(rng, dims, jnp.float32)
    if cuts:
        array = array * block_scale(rng, dims, cuts, -0.22, 0.18)
    return jnp.clip(array, -reach, reach).astype(kind)


def setup_inputs(seed: int = 0) -> dict:
    seeds = jax.random.split(jax.random.key(seed), 5)
    return {
        "t_start": scatter_about(seeds[0], (NB * BS, M), 1.0, 6.0, ((0, 32),)),
        "h_blocks": scatter_about(seeds[1], (NB, NG, HS, BS, BS), (HB * BS) ** -0.5, 0.09375, ((0, 8), (1, 4))),
        "h_cols": draw_h_cols(jax.random.fold_in(seeds[4], 71), 0),
        "t_cols": draw_t_cols(jax.random.fold_in(seeds[4], 71), 0),
    }


def apply_hamiltonian(h_blocks, h_cols, slab):
    rows3 = slab.reshape(NB, BS, M)

    def one_row(pair):
        blocks, columns = pair
        picked = rows3[columns].astype(jnp.float32)
        partial_value = jnp.einsum("gsij,gsjm->gim", blocks.astype(jnp.float32), picked)
        rounded = lax.optimization_barrier(partial_value.astype(jnp.bfloat16))
        return jnp.sum(rounded.astype(jnp.float32), axis=0)

    return lax.map(one_row, (h_blocks, h_cols))


def reference(t_start, h_blocks, h_cols, t_cols):
    kept = jnp.any(t_cols[:, :, None] == jnp.arange(MB, dtype=jnp.int32)[None, None, :], axis=1)
    keep = kept.astype(jnp.float32)[:, None, :, None]

    def masked(values):
        shaped = values.reshape(NB, BS, MB, BS) * keep
        return shaped.reshape(NB * BS, M)

    first = masked(apply_hamiltonian(h_blocks, h_cols, t_start)).astype(jnp.bfloat16)
    before, latest = t_start, first
    for step in range(STEPS - 1):
        summed = apply_hamiltonian(h_blocks, h_cols, latest).reshape(NB * BS, M)
        after = masked(2.0 * summed - before.astype(jnp.float32)).astype(jnp.bfloat16)
        before, latest = latest, after
    return before, latest
```

```python
import functools

import jax
import jax.numpy as jnp
from jax import lax
from jax.experimental import pallas as pl
from jax.experimental.pallas import tpu as pltpu
from jax.sharding import PartitionSpec as P

BS = 128
STEPS = 3
CHUNKS = 4
SUB = BS // CHUNKS
TILE = 16
MESH = pl.DeviceIdType.MESH
BF16 = jnp.bfloat16
F32 = jnp.float32
DENSE_BYTES = 8 << 20


def kernel(dims, t_hbm, h_hbm, hc, tc, before_ref, last_ref, *scratch):
    groups, rows, rb, cb, keeps, hrows, slots, dense = dims
    bufs = scratch[:STEPS]
    tv, hs, hst, hd, unp, acc, stage, landed, dgrp = scratch[STEPS : STEPS + 9]
    ag_s, ag_r, rl_s, fw_s, fw_r, rs_s, rs_r, dg_s, dg_r, local = scratch[STEPS + 9 :]
    pairs = rows // 2
    nblk = rows * rb
    full, packed = cb * SUB, keeps * SUB
    wide = rb * BS
    phases = STEPS * CHUNKS
    g = lax.axis_index("grp")
    r = lax.axis_index("row")
    pair, core = r // 2, lax.rem(r, 2)
    sibling = pair * 2 + 1 - core

    def copy(src, dst, ss, rs, row=None, grp=None):
        return pltpu.make_async_remote_copy(
            src_ref=src,
            dst_ref=dst,
            send_sem=ss,
            recv_sem=rs,
            device_id=(g if grp is None else grp, r if row is None else row),
            device_id_type=MESH,
        )

    t_copy = pltpu.make_async_copy(t_hbm, tv, local.at[0])
    t_copy.start()
    h_copy = pltpu.make_async_copy(h_hbm.at[:, 0], hs, local.at[1])
    h_copy.start()

    reach = [d for d in (2, -2, 1, -1) if abs(d) < pairs]

    def there(d):
        return (pair + d >= 0) & (pair + d < pairs)

    def at_pair(d):
        return lax.rem(pair + d + 2 * pairs, pairs) * 2 + core

    barrier = pltpu.get_barrier_semaphore()
    greeted = jnp.int32(groups)
    for k in range(1, groups):
        pl.semaphore_signal(barrier, inc=1, device_id=(lax.rem(g + k, groups), r), device_id_type=MESH)
    pl.semaphore_signal(barrier, inc=1, device_id=(g, sibling), device_id_type=MESH)
    for d in reach:

        @pl.when(there(d))
        def _():
            pl.semaphore_signal(barrier, inc=1, device_id=(g, at_pair(d)), device_id_type=MESH)

        greeted = greeted + jnp.where(there(d), 1, 0)

    lanes = []
    for b in range(rb):
        total = tc[b, 0]
        for s in range(1, keeps):
            total = total + tc[b, s]
        lanes.append(jnp.full((TILE, BS), cb * (cb - 1) // 2 - total, jnp.int32).astype(F32).astype(BF16))
    mark = jnp.concatenate(lanes, axis=1)
    dgrp[g] = mark
    bufs[0][0, r, full:, :] = mark
    t_copy.wait()
    turned = tv[...].T
    for q in range(CHUNKS):
        for c in range(cb):
            at = c * BS + q * SUB
            bufs[0][q, r, c * SUB : (c + 1) * SUB, :] = turned[at : at + SUB, :]
    pl.semaphore_wait(barrier, greeted)

    sends = [[] for _ in range(phases)]

    def go(phase, one, cond=None):
        if cond is None:
            one.start()
        else:
            pl.when(cond)(one.start)
        sends[phase].append((one, cond))

    def drain(phase):
        for one, cond in sends[phase]:
            if cond is None:
                one.wait_send()
            else:
                pl.when(cond)(one.wait_send)

    def piece(phase, who):
        step, q = divmod(phase, CHUNKS)
        if step:
            return bufs[step].at[q, who]
        return bufs[0].at[q, who] if q == 0 else bufs[0].at[q, who, pl.ds(0, full)]

    def gather_start(phase):
        own = piece(phase, r)
        for n, d in enumerate(reach):
            go(phase, copy(own, own, ag_s.at[phase, n], ag_r.at[phase, pair], row=at_pair(d)), there(d))
        go(phase, copy(own, own, fw_s.at[phase, 0], fw_r.at[phase, pair], row=sibling))

    inner = jnp.minimum(pair, pairs - 1 - pair)
    side = jnp.where(pair * 2 < pairs, 1, -1)

    def kth(k):
        both = k <= 2 * inner
        apart = jnp.where(both, (k + 1) // 2, k - inner)
        toward = jnp.where(both & (k % 2 == 1), -side, side)
        return pair + toward * apart, apart, toward

    order = [kth(k) for k in range(1, pairs)]

    for k in range(1, groups):
        go(0, copy(dgrp.at[g], dgrp.at[g], dg_s.at[k], dg_r.at[k], grp=lax.rem(g + k, groups)))
    gather_start(0)
    gather_start(1)

    h_copy.wait()
    for b in range(hrows):
        turned = hs[b].reshape(slots * BS, BS).T
        for s in range(slots):
            hst[b, s] = turned[:, s * BS : (s + 1) * BS]
        if dense:
            hst[b, slots] = jnp.zeros((BS, BS), BF16)
    if dense:
        for b in range(hrows):

            def build(c, carry):
                named = (c // rb) * (groups * rb) + g * rb + lax.rem(c, rb)
                at = jnp.int32(slots)
                for s in range(slots):
                    at = jnp.where(hc[b, 0, s] == named, s, at)
                hd[c, :, b * BS : (b + 1) * BS] = hst[b, at]
                return carry

            lax.fori_loop(0, nblk, build, 0)

    def tall(tile):
        return jnp.concatenate([tile] * (SUB // TILE), axis=0)

    def gone_of(who):
        return tall(bufs[0][0, who, full:, :])

    def part(c):
        return slice(c * SUB, (c + 1) * SUB)

    def unpacked(gone, value):
        zero = jnp.zeros((SUB, wide), BF16)
        out = []
        for c in range(cb):
            if c == 0:
                one = value(0)
            elif c == cb - 1:
                one = value(c - 1)
            else:
                one = jnp.where(gone < c, value(c - 1), value(c))
            out.append(jnp.where(gone == c, zero, one))
        return jnp.concatenate(out, axis=0)

    def operand(phase, who):
        step, q = divmod(phase, CHUNKS)
        if step == 0:
            return bufs[0][q, who, :full, :]
        return unpacked(gone_of(who), lambda p: bufs[step][q, who, part(p), :])

    def multiply(phase, src, first):
        both = [operand(phase, src * 2 + n) for n in range(2)]
        if not dense:
            for n in range(2):
                for b in range(rb):
                    unp[(src * 2 + n) * rb + b] = both[n][:, b * BS : (b + 1) * BS]
            return
        right = hd[pl.ds(src * 2 * rb, 2 * rb)].reshape(2 * wide, hrows * BS)
        out = jnp.dot(jnp.concatenate(both, axis=1), right, preferred_element_type=F32)
        for k in range(groups):
            value = out[:, k * wide : (k + 1) * wide]
            acc[k] = value if first else acc[k] + value

    def multiply_sparse():
        def one_group(k, carry):
            for b in range(rb):
                i = k * rb + b
                out = jnp.zeros((full, BS), F32)
                for s in range(slots):
                    named = hc[i, 0, s]
                    at = named // (groups * rb) * rb + lax.rem(named, rb)
                    out = out + jnp.dot(unp[at], hst[i, s], preferred_element_type=F32)
                acc[k, :, b * BS : (b + 1) * BS] = out
            return carry

        lax.fori_loop(0, groups, one_group, 0)

    def gather_multiply(phase, then=None):
        def forwarded(src):
            got = piece(phase, src * 2 + 1 - core)
            copy(got, got, fw_s.at[phase, 0], fw_r.at[phase, src], row=sibling).wait_recv()

        before = pair
        for n, (src, apart, toward) in enumerate(order):
            got = piece(phase, src * 2 + core)
            copy(got, got, fw_s.at[phase, 0], ag_r.at[phase, src], row=sibling).wait_recv()
            if n + 1 >= 2:
                go(
                    phase,
                    copy(got, got, rl_s.at[phase, n], ag_r.at[phase, src], row=lax.rem(pair - toward + pairs, pairs) * 2 + core),
                    (apart >= 2) & (pair - toward >= 0) & (pair - toward < pairs),
                )
            go(phase, copy(got, got, fw_s.at[phase, n + 1], fw_r.at[phase, src], row=sibling))
            forwarded(before)
            multiply(phase, before, n == 0)
            before = src
        if then is not None:
            then()
        forwarded(before)
        multiply(phase, before, pairs == 1)
        if not dense:
            multiply_sparse()

    def scatter_start(phase):
        for k in range(1, groups + 1):
            to = lax.rem(g + k, groups)
            gone = tall(dgrp[to])
            for p in range(keeps):
                low, high = acc[to, part(p), :].astype(BF16), acc[to, part(p + 1), :].astype(BF16)
                stage[phase, to, part(p), :] = jnp.where(gone > p, low, high)
            if k < groups:
                go(phase, copy(stage.at[phase, to], landed.at[phase, g], rs_s.at[phase, k], rs_r.at[phase, k], grp=to))

    def scatter_finish(phase):
        step, q = divmod(phase, CHUNKS)
        for k in range(1, groups):
            got = landed.at[phase, lax.rem(g + groups - k, groups)]
            copy(got, got, rs_s.at[phase, k], rs_r.at[phase, k], row=sibling).wait_recv()
        gone = tall(dgrp[g])
        for p in range(keeps):
            new = stage[phase, g, part(p), :].astype(F32)
            for k in range(1, groups):
                new = new + landed[phase, lax.rem(g + k, groups), part(p), :].astype(F32)
            if step == 1:
                old = jnp.where(gone > p, bufs[0][q, r, part(p), :], bufs[0][q, r, part(p + 1), :])
                new = 2.0 * new - old.astype(F32)
            elif step > 1:
                new = 2.0 * new - bufs[step - 1][q, r, part(p), :].astype(F32)
            if step < STEPS - 1:
                bufs[step + 1][q, r, part(p), :] = new.astype(BF16)
            else:
                stage[phase, g, part(p), :] = new.astype(BF16)
        if step < STEPS - 1:
            gather_start(phase + CHUNKS)

    def deliver(ref, source):
        gone = tall(dgrp[g])
        pieces = [unpacked(gone, lambda p: source(q, p)) for q in range(CHUNKS)]
        whole = jnp.concatenate([pieces[q][part(c), :] for c in range(cb) for q in range(CHUNKS)], axis=0)
        ref[...] = whole.T

    for phase in range(phases):
        ahead = phase + 2 if phase + 2 < CHUNKS else None
        gather_multiply(phase, None if ahead is None else functools.partial(gather_start, ahead))
        if phase == 0:
            for k in range(1, groups):
                got = dgrp.at[lax.rem(g + groups - k, groups)]
                copy(got, got, dg_s.at[k], dg_r.at[k], row=sibling).wait_recv()
        scatter_start(phase)
        if phase:
            scatter_finish(phase - 1)
        if phase >= 3:
            drain(phase - 3)
    deliver(before_ref, lambda q, p: bufs[STEPS - 1][q, r, part(p), :])
    scatter_finish(phases - 1)
    deliver(last_ref, lambda q, p: stage[(STEPS - 1) * CHUNKS + q, g, part(p), :])
    for phase in range(phases - 3, phases):
        drain(phase)


def per_device(t_start, h_blocks, h_cols, t_cols):
    groups, rows = lax.axis_size("grp"), lax.axis_size("row")
    rb, cb = t_start.shape[0] // BS, t_start.shape[1] // BS
    hrows, slots = h_blocks.shape[0], h_blocks.shape[2]
    keeps = t_cols.shape[1]
    nblk = rows * rb
    pairs = rows // 2
    wide = rb * BS
    dense = hrows * nblk * BS * BS * 2 <= DENSE_BYTES
    phases = STEPS * CHUNKS
    dma = pltpu.SemaphoreType.DMA
    out = jax.ShapeDtypeStruct(t_start.shape, t_start.dtype)
    return pl.pallas_call(
        functools.partial(kernel, (groups, rows, rb, cb, keeps, hrows, slots, dense)),
        out_shape=(out, out),
        in_specs=[
            pl.BlockSpec(memory_space=pl.ANY),
            pl.BlockSpec(memory_space=pl.ANY),
            pl.BlockSpec(memory_space=pltpu.SMEM),
            pl.BlockSpec(memory_space=pltpu.SMEM),
        ],
        out_specs=(pl.BlockSpec(memory_space=pltpu.VMEM),) * 2,
        scratch_shapes=[
            pltpu.VMEM((CHUNKS, rows, cb * SUB + TILE, wide), BF16),
            *[pltpu.VMEM((CHUNKS, rows, keeps * SUB, wide), BF16) for _ in range(STEPS - 1)],
            pltpu.VMEM(t_start.shape, BF16),
            pltpu.VMEM((hrows, slots, BS, BS), BF16),
            pltpu.VMEM((hrows, slots + 1, BS, BS), BF16),
            pltpu.VMEM((nblk, BS, hrows * BS) if dense else (1, TILE, BS), BF16),
            pltpu.VMEM((1, TILE, BS) if dense else (nblk, cb * SUB, BS), BF16),
            pltpu.VMEM((groups, cb * SUB, wide), F32),
            pltpu.VMEM((phases, groups, keeps * SUB, wide), BF16),
            pltpu.VMEM((phases, groups, keeps * SUB, wide), BF16),
            pltpu.VMEM((groups, TILE, wide), BF16),
            dma((phases, 4)),
            dma((phases, pairs)),
            dma((phases, pairs)),
            dma((phases, pairs)),
            dma((phases, pairs)),
            dma((phases, groups)),
            dma((phases, groups)),
            dma((groups,)),
            dma((groups,)),
            dma((2,)),
        ],
        compiler_params=pltpu.CompilerParams(
            collective_id=0, has_side_effects=True, vmem_limit_bytes=56 << 20
        ),
    )(t_start, h_blocks, h_cols, t_cols)


def solution(mesh):
    placed = (
        P(("row", "grp"), None),
        P("row", "grp", None, None, None),
        P("row", "grp", None),
        P(("row", "grp"), None),
    )
    return jax.shard_map(
        per_device,
        mesh=mesh,
        in_specs=placed,
        out_specs=(P(("row", "grp"), None), P(("row", "grp"), None)),
        check_vma=False,
    )
```

```python
import functools

import jax
import jax.numpy as jnp
from jax import lax
from jax.experimental import pallas as pl
from jax.experimental.pallas import tpu as pltpu
from jax.sharding import PartitionSpec as P

BS = 128
STEPS = 3
CHUNKS = 4
SUB = BS // CHUNKS
TILE = 16
MESH = pl.DeviceIdType.MESH
BF16 = jnp.bfloat16
F32 = jnp.float32
DENSE_BYTES = 8 << 20
AHEAD = 4


def kernel(dims, t_hbm, h_hbm, hc, tc, before_ref, last_ref, *scratch):
    groups, rows, rb, cb, keeps, hrows, slots, dense = dims
    bufs = scratch[:STEPS]
    tv, hs, hst, hd, unp, acc, stage, landed, dgrp = scratch[STEPS : STEPS + 9]
    ag_s, ag_r, rl_s, fw_s, fw_r, rs_s, rs_r, dg_s, dg_r, local = scratch[STEPS + 9 :]
    pairs = rows // 2
    nblk = rows * rb
    full, packed = cb * SUB, keeps * SUB
    wide = rb * BS
    phases = STEPS * CHUNKS
    g = lax.axis_index("grp")
    r = lax.axis_index("row")
    pair, core = r // 2, lax.rem(r, 2)
    sibling = pair * 2 + 1 - core

    def copy(src, dst, ss, rs, row=None, grp=None):
        return pltpu.make_async_remote_copy(
            src_ref=src,
            dst_ref=dst,
            send_sem=ss,
            recv_sem=rs,
            device_id=(g if grp is None else grp, r if row is None else row),
            device_id_type=MESH,
        )

    t_copy = pltpu.make_async_copy(t_hbm, tv, local.at[0])
    t_copy.start()
    h_copy = pltpu.make_async_copy(h_hbm.at[:, 0], hs, local.at[1])
    h_copy.start()

    reach = [d for d in (1, -1, 2, -2) if abs(d) < pairs]

    def inside(d):
        return (pair + d >= 0) & (pair + d < pairs)

    def there(d):
        if abs(d) == 1:
            return inside(d)
        return (pair + d > 0) & (pair + d < pairs - 1)

    def at_pair(d):
        return lax.rem(pair + d + 2 * pairs, pairs) * 2 + core

    barrier = pltpu.get_barrier_semaphore()
    greeted = jnp.int32(groups)
    for k in range(1, groups):
        pl.semaphore_signal(barrier, inc=1, device_id=(lax.rem(g + k, groups), r), device_id_type=MESH)
    pl.semaphore_signal(barrier, inc=1, device_id=(g, sibling), device_id_type=MESH)
    for d in reach:

        @pl.when(inside(d))
        def _():
            pl.semaphore_signal(barrier, inc=1, device_id=(g, at_pair(d)), device_id_type=MESH)

        greeted = greeted + jnp.where(inside(d), 1, 0)

    lanes = []
    for b in range(rb):
        total = tc[b, 0]
        for s in range(1, keeps):
            total = total + tc[b, s]
        lanes.append(jnp.full((TILE, BS), cb * (cb - 1) // 2 - total, jnp.int32).astype(F32).astype(BF16))
    mark = jnp.concatenate(lanes, axis=1)
    dgrp[g] = mark
    bufs[0][0, r, full:, :] = mark
    t_copy.wait()
    turned = tv[...].T
    for q in range(CHUNKS):
        for c in range(cb):
            at = c * BS + q * SUB
            bufs[0][q, r, c * SUB : (c + 1) * SUB, :] = turned[at : at + SUB, :]
    pl.semaphore_wait(barrier, greeted)

    sends = [[] for _ in range(phases)]

    def go(phase, one, cond=None):
        if cond is None:
            one.start()
        else:
            pl.when(cond)(one.start)
        sends[phase].append((one, cond))

    def drain(phase):
        for one, cond in sends[phase]:
            if cond is None:
                one.wait_send()
            else:
                pl.when(cond)(one.wait_send)

    def piece(phase, who):
        step, q = divmod(phase, CHUNKS)
        if step:
            return bufs[step].at[q, who]
        return bufs[0].at[q, who] if q == 0 else bufs[0].at[q, who, pl.ds(0, full)]

    def gather_start(phase):
        own = piece(phase, r)
        for n, d in enumerate(reach):
            go(phase, copy(own, own, ag_s.at[phase, n], ag_r.at[phase, pair], row=at_pair(d)), there(d))
        go(phase, copy(own, own, fw_s.at[phase, 0], fw_r.at[phase, pair], row=sibling))

    inner = jnp.minimum(pair, pairs - 1 - pair)
    side = jnp.where(pair * 2 < pairs, 1, -1)

    def kth(k):
        both = k <= 2 * inner
        apart = jnp.where(both, (k + 1) // 2, k - inner)
        toward = jnp.where(both & (k % 2 == 1), -side, side)
        return pair + toward * apart, apart, toward

    order = [kth(k) for k in range(1, pairs)]

    for k in range(1, groups):
        go(0, copy(dgrp.at[g], dgrp.at[g], dg_s.at[k], dg_r.at[k], grp=lax.rem(g + k, groups)))
    for q in range(AHEAD):
        gather_start(q)

    def turn_blocks():
        h_copy.wait()
        for b in range(hrows):
            turned = hs[b].reshape(slots * BS, BS).T
            for s in range(slots):
                hst[b, s] = turned[:, s * BS : (s + 1) * BS]
            if dense:
                hst[b, slots] = jnp.zeros((BS, BS), BF16)

    def lay_out():
        def build(c, carry):
            named = (c // rb) * (groups * rb) + g * rb + lax.rem(c, rb)
            for b in range(hrows):
                at = jnp.int32(slots)
                for s in range(slots):
                    at = jnp.where(hc[b, 0, s] == named, s, at)
                hd[c, :, b * BS : (b + 1) * BS] = hst[b, at]
            return carry

        lax.fori_loop(0, nblk, build, 0)

    def tall(tile):
        return jnp.concatenate([tile] * (SUB // TILE), axis=0)

    def gone_of(who):
        return tall(bufs[0][0, who, full:, :])

    def part(c):
        return slice(c * SUB, (c + 1) * SUB)

    def unpacked(gone, value):
        zero = jnp.zeros((SUB, wide), BF16)
        out = []
        for c in range(cb):
            if c == 0:
                one = value(0)
            elif c == cb - 1:
                one = value(c - 1)
            else:
                one = jnp.where(gone < c, value(c - 1), value(c))
            out.append(jnp.where(gone == c, zero, one))
        return jnp.concatenate(out, axis=0)

    def operand(phase, who):
        step, q = divmod(phase, CHUNKS)
        if step == 0:
            return bufs[0][q, who, :full, :]
        return unpacked(gone_of(who), lambda p: bufs[step][q, who, part(p), :])

    def multiply(phase, src, first):
        both = [operand(phase, src * 2 + n) for n in range(2)]
        if not dense:
            for n in range(2):
                for b in range(rb):
                    unp[(src * 2 + n) * rb + b] = both[n][:, b * BS : (b + 1) * BS]
            return
        right = hd[pl.ds(src * 2 * rb, 2 * rb)].reshape(2 * wide, hrows * BS)
        out = jnp.dot(jnp.concatenate(both, axis=1), right, preferred_element_type=F32)
        for k in range(groups):
            value = out[:, k * wide : (k + 1) * wide]
            acc[k] = value if first else acc[k] + value

    def multiply_sparse():
        def one_group(k, carry):
            for b in range(rb):
                i = k * rb + b
                out = jnp.zeros((full, BS), F32)
                for s in range(slots):
                    named = hc[i, 0, s]
                    at = named // (groups * rb) * rb + lax.rem(named, rb)
                    out = out + jnp.dot(unp[at], hst[i, s], preferred_element_type=F32)
                acc[k, :, b * BS : (b + 1) * BS] = out
            return carry

        lax.fori_loop(0, groups, one_group, 0)

    def forwarded(phase, src):
        got = piece(phase, src * 2 + 1 - core)
        copy(got, got, fw_s.at[phase, 0], fw_r.at[phase, src], row=sibling).wait_recv()

    def pass_on(phase, n):
        src, apart, toward = order[n]
        got = piece(phase, src * 2 + core)
        copy(got, got, fw_s.at[phase, 0], ag_r.at[phase, src], row=sibling).wait_recv()
        beyond = pair - toward
        go(
            phase,
            copy(got, got, rl_s.at[phase, n], ag_r.at[phase, src], row=lax.rem(beyond + pairs, pairs) * 2 + core),
            ((apart >= 2) | (beyond == 0) | (beyond == pairs - 1)) & (beyond >= 0) & (beyond < pairs),
        )
        go(phase, copy(got, got, fw_s.at[phase, n + 1], fw_r.at[phase, src], row=sibling))

    def gather_multiply(phase, done=0, then=None):
        before = pair
        for n, (src, _, _) in enumerate(order):
            if n >= done:
                pass_on(phase, n)
            forwarded(phase, before)
            multiply(phase, before, n == 0)
            before = src
        if then is not None:
            then()
        forwarded(phase, before)
        multiply(phase, before, pairs == 1)
        if not dense:
            multiply_sparse()

    def scatter_start(phase):
        for k in range(1, groups + 1):
            to = lax.rem(g + k, groups)
            gone = tall(dgrp[to])
            for p in range(keeps):
                low, high = acc[to, part(p), :].astype(BF16), acc[to, part(p + 1), :].astype(BF16)
                stage[phase, to, part(p), :] = jnp.where(gone > p, low, high)
            if k < groups:
                go(phase, copy(stage.at[phase, to], landed.at[phase, g], rs_s.at[phase, k], rs_r.at[phase, k], grp=to))

    def scatter_finish(phase):
        step, q = divmod(phase, CHUNKS)
        for k in range(1, groups):
            got = landed.at[phase, lax.rem(g + groups - k, groups)]
            copy(got, got, rs_s.at[phase, k], rs_r.at[phase, k], row=sibling).wait_recv()
        gone = tall(dgrp[g])
        for p in range(keeps):
            new = stage[phase, g, part(p), :].astype(F32)
            for k in range(1, groups):
                new = new + landed[phase, lax.rem(g + k, groups), part(p), :].astype(F32)
            if step == 1:
                old = jnp.where(gone > p, bufs[0][q, r, part(p), :], bufs[0][q, r, part(p + 1), :])
                new = 2.0 * new - old.astype(F32)
            elif step > 1:
                new = 2.0 * new - bufs[step - 1][q, r, part(p), :].astype(F32)
            if step < STEPS - 1:
                bufs[step + 1][q, r, part(p), :] = new.astype(BF16)
            else:
                stage[phase, g, part(p), :] = new.astype(BF16)
        if step < STEPS - 1:
            gather_start(phase + CHUNKS)

    def deliver(ref, source):
        gone = tall(dgrp[g])
        pieces = [unpacked(gone, lambda p: source(q, p)) for q in range(CHUNKS)]
        whole = jnp.concatenate([pieces[q][part(c), :] for c in range(cb) for q in range(CHUNKS)], axis=0)
        ref[...] = whole.T

    turn_blocks()
    early = min(2, len(order))
    for n in range(early):
        pass_on(0, n)
    if dense:
        lay_out()
    for phase in range(phases):
        ahead = phase + AHEAD if phase + AHEAD < CHUNKS else None
        gather_multiply(phase, early, None if ahead is None else functools.partial(gather_start, ahead))
        if phase == 0:
            for k in range(1, groups):
                got = dgrp.at[lax.rem(g + groups - k, groups)]
                copy(got, got, dg_s.at[k], dg_r.at[k], row=sibling).wait_recv()
        scatter_start(phase)
        if phase + 1 < phases and True:
            for n in range(early):
                pass_on(phase + 1, n)
        if phase:
            scatter_finish(phase - 1)
        if phase >= 3:
            drain(phase - 3)
    deliver(before_ref, lambda q, p: bufs[STEPS - 1][q, r, part(p), :])
    scatter_finish(phases - 1)
    deliver(last_ref, lambda q, p: stage[(STEPS - 1) * CHUNKS + q, g, part(p), :])
    for phase in range(phases - 3, phases):
        drain(phase)


def per_device(t_start, h_blocks, h_cols, t_cols):
    groups, rows = lax.axis_size("grp"), lax.axis_size("row")
    rb, cb = t_start.shape[0] // BS, t_start.shape[1] // BS
    hrows, slots = h_blocks.shape[0], h_blocks.shape[2]
    keeps = t_cols.shape[1]
    nblk = rows * rb
    pairs = rows // 2
    wide = rb * BS
    dense = hrows * nblk * BS * BS * 2 <= DENSE_BYTES
    phases = STEPS * CHUNKS
    dma = pltpu.SemaphoreType.DMA
    out = pltpu.VMEM(t_start.shape, t_start.dtype)
    return pl.pallas_call(
        functools.partial(kernel, (groups, rows, rb, cb, keeps, hrows, slots, dense)),
        out_shape=(out, out),
        in_specs=[
            pl.BlockSpec(memory_space=pl.ANY),
            pl.BlockSpec(memory_space=pl.ANY),
            pl.BlockSpec(memory_space=pltpu.SMEM),
            pl.BlockSpec(memory_space=pltpu.SMEM),
        ],
        out_specs=(pl.BlockSpec(memory_space=pltpu.VMEM),) * 2,
        scratch_shapes=[
            pltpu.VMEM((CHUNKS, rows, cb * SUB + TILE, wide), BF16),
            *[pltpu.VMEM((CHUNKS, rows, keeps * SUB, wide), BF16) for _ in range(STEPS - 1)],
            pltpu.VMEM(t_start.shape, BF16),
            pltpu.VMEM((hrows, slots, BS, BS), BF16),
            pltpu.VMEM((hrows, slots + 1, BS, BS), BF16),
            pltpu.VMEM((nblk, BS, hrows * BS) if dense else (1, TILE, BS), BF16),
            pltpu.VMEM((1, TILE, BS) if dense else (nblk, cb * SUB, BS), BF16),
            pltpu.VMEM((groups, cb * SUB, wide), F32),
            pltpu.VMEM((phases, groups, keeps * SUB, wide), BF16),
            pltpu.VMEM((phases, groups, keeps * SUB, wide), BF16),
            pltpu.VMEM((groups, TILE, wide), BF16),
            dma((phases, 4)),
            dma((phases, pairs)),
            dma((phases, pairs)),
            dma((phases, pairs)),
            dma((phases, pairs)),
            dma((phases, groups)),
            dma((phases, groups)),
            dma((groups,)),
            dma((groups,)),
            dma((2,)),
        ],
        compiler_params=pltpu.CompilerParams(
            collective_id=0, has_side_effects=True, vmem_limit_bytes=56 << 20
        ),
    )(t_start, h_blocks, h_cols, t_cols)


def solution(mesh):
    placed = (
        P(("row", "grp"), None),
        P("row", "grp", None, None, None),
        P("row", "grp", None),
        P(("row", "grp"), None),
    )
    return jax.shard_map(
        per_device,
        mesh=mesh,
        in_specs=placed,
        out_specs=(P(("row", "grp"), None), P(("row", "grp"), None)),
        check_vma=False,
    )
```

```python
import functools

import jax
import jax.numpy as jnp
from jax import lax
from jax.experimental import pallas as pl
from jax.experimental.pallas import tpu as pltpu
from jax.sharding import PartitionSpec as P

BS = 128
STEPS = 3
SIZES = (32, 32, 32, 32)
CHUNKS = len(SIZES)
FROM = tuple(sum(SIZES[:q]) for q in range(CHUNKS))
WIDEST = max(SIZES)
TILE = 16
MESH = pl.DeviceIdType.MESH
BF16 = jnp.bfloat16
F32 = jnp.float32
DENSE_BYTES = 8 << 20
AHEAD = 3


def kernel(dims, t_hbm, h_hbm, hc_hbm, tc_hbm, before_ref, last_ref, *scratch):
    groups, rows, rb, cb, keeps, hrows, slots, dense = dims
    bufs = scratch[:STEPS]
    tv, hs, hst, hd, unp, acc, stage, landed, dgrp, hc, tc = scratch[STEPS : STEPS + 11]
    ag_s, ag_r, rl_s, fw_s, fw_r, rs_s, rs_r, dg_s, dg_r, local = scratch[STEPS + 11 :]
    pairs = rows // 2
    nblk = rows * rb
    full = [cb * size for size in SIZES]
    packed = [keeps * size for size in SIZES]
    wide = rb * BS
    phases = STEPS * CHUNKS
    g = lax.axis_index("grp")
    r = lax.axis_index("row")
    pair, core = r // 2, lax.rem(r, 2)
    sibling = pair * 2 + 1 - core

    def part(q, c):
        return slice(c * SIZES[q], (c + 1) * SIZES[q])

    def copy(src, dst, ss, rs, row=None, grp=None):
        return pltpu.make_async_remote_copy(
            src_ref=src,
            dst_ref=dst,
            send_sem=ss,
            recv_sem=rs,
            device_id=(g if grp is None else grp, r if row is None else row),
            device_id_type=MESH,
        )

    t_copy = pltpu.make_async_copy(t_hbm, tv, local.at[0])
    t_copy.start()
    tc_copy = pltpu.make_async_copy(tc_hbm, tc, local.at[1])
    tc_copy.start()
    reach = [d for d in (2, -2, 1, -1) if abs(d) < pairs]

    def inside(d):
        return (pair + d >= 0) & (pair + d < pairs)

    def partner(k):
        other = g
        for i in range(groups.bit_length() - 1):
            if k >> i & 1:
                other = other + (1 - 2 * lax.rem(g // (1 << i), 2)) * (1 << i)
        return other

    def there(d):
        if abs(d) == 1:
            return inside(d)
        return (pair + d > 0) & (pair + d < pairs - 1)

    def at_pair(d):
        return lax.rem(pair + d + 2 * pairs, pairs) * 2 + core

    barrier = pltpu.get_barrier_semaphore()
    greeted = jnp.int32(groups)
    for k in range(1, groups):
        pl.semaphore_signal(barrier, inc=1, device_id=(partner(k), r), device_id_type=MESH)
    pl.semaphore_signal(barrier, inc=1, device_id=(g, sibling), device_id_type=MESH)
    for d in reach:

        @pl.when(inside(d))
        def _():
            pl.semaphore_signal(barrier, inc=1, device_id=(g, at_pair(d)), device_id_type=MESH)

        greeted = greeted + jnp.where(inside(d), 1, 0)

    h_copy = pltpu.make_async_copy(h_hbm.at[:, 0], hs, local.at[2])
    h_copy.start()
    hc_copy = pltpu.make_async_copy(hc_hbm, hc, local.at[3])
    hc_copy.start()
    tc_copy.wait()
    lanes = []
    for b in range(rb):
        total = tc[b, 0]
        for s in range(1, keeps):
            total = total + tc[b, s]
        lanes.append(jnp.full((TILE, BS), cb * (cb - 1) // 2 - total, jnp.int32).astype(F32).astype(BF16))
    mark = jnp.concatenate(lanes, axis=1)
    dgrp[g] = mark
    bufs[0][0, r, full[0] : full[0] + TILE, :] = mark
    t_copy.wait()
    turned = tv[...].T
    for q in range(CHUNKS):
        for c in range(cb):
            at = c * BS + FROM[q]
            bufs[0][q, r, part(q, c), :] = turned[at : at + SIZES[q], :]
    pl.semaphore_wait(barrier, greeted)

    sends = [[] for _ in range(phases)]

    def go(phase, one, cond=None):
        if cond is None:
            one.start()
        else:
            pl.when(cond)(one.start)
        sends[phase].append((one, cond))

    def drain(phase):
        for one, cond in sends[phase]:
            if cond is None:
                one.wait_send()
            else:
                pl.when(cond)(one.wait_send)

    def piece(phase, who):
        step, q = divmod(phase, CHUNKS)
        if step:
            return bufs[step].at[q, who, pl.ds(0, packed[q])]
        return bufs[0].at[q, who, pl.ds(0, full[q] + (0 if q else TILE))]

    def gather_start(phase):
        own = piece(phase, r)
        for n, d in enumerate(reach):
            go(phase, copy(own, own, ag_s.at[phase, n], ag_r.at[phase, pair], row=at_pair(d)), there(d))
        go(phase, copy(own, own, fw_s.at[phase, 0], fw_r.at[phase, pair], row=sibling))

    def ranked(p):
        far = 1 if 2 * p < pairs else -1
        short = lambda s: pairs == 4 and (s - p) * far < 0
        return sorted((s for s in range(pairs) if s != p), key=lambda s: (short(s), abs(s - p), (s - p) * far < 0))

    def kth(n):
        src = jnp.int32(ranked(0)[n])
        for p in range(1, pairs):
            src = jnp.where(pair == p, ranked(p)[n], src)
        toward = jnp.where(src > pair, 1, -1)
        return src, (src - pair) * toward, toward

    order = [kth(n) for n in range(pairs - 1)]

    for k in range(1, groups):
        go(0, copy(dgrp.at[g], dgrp.at[g], dg_s.at[k], dg_r.at[k], grp=partner(k)))
    for q in range(AHEAD):
        gather_start(q)

    def turn_blocks():
        h_copy.wait()
        hc_copy.wait()
        for b in range(hrows):
            turned = hs[b].reshape(slots * BS, BS).T
            for s in range(slots):
                hst[b, s] = turned[:, s * BS : (s + 1) * BS]
            if dense:
                hst[b, slots] = jnp.zeros((BS, BS), BF16)

    def lay_out():
        def build(c, carry):
            named = (c // rb) * (groups * rb) + g * rb + lax.rem(c, rb)
            for b in range(hrows):
                at = jnp.int32(slots)
                for s in range(slots):
                    at = jnp.where(hc[b, 0, s] == named, s, at)
                hd[c, :, b * BS : (b + 1) * BS] = hst[b, at]
            return carry

        lax.fori_loop(0, nblk, build, 0)

    def tall(q, tile):
        return jnp.concatenate([tile] * (SIZES[q] // TILE), axis=0)

    def gone_of(q, who):
        return tall(q, bufs[0][0, who, full[0] : full[0] + TILE, :])

    def unpacked(gone, value):
        zero = jnp.zeros(gone.shape, BF16)
        out = []
        for c in range(cb):
            if c == 0:
                one = value(0)
            elif c == cb - 1:
                one = value(c - 1)
            else:
                one = jnp.where(gone < c, value(c - 1), value(c))
            out.append(jnp.where(gone == c, zero, one))
        return jnp.concatenate(out, axis=0)

    def operand(phase, who):
        step, q = divmod(phase, CHUNKS)
        if step == 0:
            return bufs[0][q, who, : full[q], :]
        return unpacked(gone_of(q, who), lambda p: bufs[step][q, who, part(q, p), :])

    def multiply(phase, src, first):
        both = [operand(phase, src * 2 + n) for n in range(2)]
        high = full[phase % CHUNKS]
        if not dense:
            for n in range(2):
                for b in range(rb):
                    unp[(src * 2 + n) * rb + b, :high] = both[n][:, b * BS : (b + 1) * BS]
            return
        right = hd[pl.ds(src * 2 * rb, 2 * rb)].reshape(2 * wide, hrows * BS)
        out = jnp.dot(jnp.concatenate(both, axis=1), right, preferred_element_type=F32)
        for k in range(groups):
            value = out[:, k * wide : (k + 1) * wide]
            acc[k, :high] = value if first else acc[k, :high] + value

    def multiply_sparse(phase):
        high = full[phase % CHUNKS]

        def one_group(k, carry):
            for b in range(rb):
                i = k * rb + b
                out = jnp.zeros((high, BS), F32)
                for s in range(slots):
                    named = hc[i, 0, s]
                    at = named // (groups * rb) * rb + lax.rem(named, rb)
                    out = out + jnp.dot(unp[at][:high], hst[i, s], preferred_element_type=F32)
                acc[k, :high, b * BS : (b + 1) * BS] = out
            return carry

        lax.fori_loop(0, groups, one_group, 0)

    def forwarded(phase, src):
        got = piece(phase, src * 2 + 1 - core)
        copy(got, got, fw_s.at[phase, 0], fw_r.at[phase, src], row=sibling).wait_recv()

    def pass_on(phase, n):
        src, apart, toward = order[n]
        got = piece(phase, src * 2 + core)
        copy(got, got, fw_s.at[phase, 0], ag_r.at[phase, src], row=sibling).wait_recv()
        beyond = pair - toward
        go(
            phase,
            copy(got, got, rl_s.at[phase, n], ag_r.at[phase, src], row=lax.rem(beyond + pairs, pairs) * 2 + core),
            ((apart >= 2) | (beyond == 0) | (beyond == pairs - 1)) & (beyond >= 0) & (beyond < pairs),
        )
        go(phase, copy(got, got, fw_s.at[phase, n + 1], fw_r.at[phase, src], row=sibling))

    def gather_multiply(phase, done):
        before = pair
        for n, (src, _, _) in enumerate(order):
            if n >= done:
                pass_on(phase, n)
            forwarded(phase, before)
            multiply(phase, before, n == 0)
            before = src
        forwarded(phase, before)
        multiply(phase, before, pairs == 1)
        if not dense:
            multiply_sparse(phase)

    def scatter_start(phase):
        q = phase % CHUNKS
        rows_here = pl.ds(0, packed[q])
        for k in [*range(groups - 1, 0, -1), 0]:
            to = partner(k)
            gone = tall(q, dgrp[to])
            for p in range(keeps):
                low, high = acc[to, part(q, p), :].astype(BF16), acc[to, part(q, p + 1), :].astype(BF16)
                stage[phase, to, part(q, p), :] = jnp.where(gone > p, low, high)
            if k:
                go(phase, copy(stage.at[phase, to, rows_here], landed.at[phase, g, rows_here], rs_s.at[phase, k], rs_r.at[phase, k], grp=to))

    def scatter_finish(phase):
        step, q = divmod(phase, CHUNKS)
        for k in range(1, groups):
            got = landed.at[phase, partner(k), pl.ds(0, packed[q])]
            copy(got, got, rs_s.at[phase, k], rs_r.at[phase, k], row=sibling).wait_recv()
        gone = tall(q, dgrp[g])
        for p in range(keeps):
            new = stage[phase, g, part(q, p), :].astype(F32)
            for k in range(1, groups):
                new = new + landed[phase, partner(k), part(q, p), :].astype(F32)
            if step == 1:
                old = jnp.where(gone > p, bufs[0][q, r, part(q, p), :], bufs[0][q, r, part(q, p + 1), :])
                new = 2.0 * new - old.astype(F32)
            elif step > 1:
                new = 2.0 * new - bufs[step - 1][q, r, part(q, p), :].astype(F32)
            if step < STEPS - 1:
                bufs[step + 1][q, r, part(q, p), :] = new.astype(BF16)
            else:
                stage[phase, g, part(q, p), :] = new.astype(BF16)
        if step < STEPS - 1:
            gather_start(phase + CHUNKS)

    def deliver(ref, source):
        pieces = [unpacked(tall(q, dgrp[g]), functools.partial(source, q)) for q in range(CHUNKS)]
        whole = jnp.concatenate([pieces[q][part(q, c), :] for c in range(cb) for q in range(CHUNKS)], axis=0)
        ref[...] = whole.T

    turn_blocks()
    early = min(2, len(order))
    for n in range(early):
        pass_on(0, n)
    for q in range(AHEAD, CHUNKS):
        gather_start(q)
    if dense:
        lay_out()
    for phase in range(phases):
        gather_multiply(phase, early)
        if phase == 0:
            for k in range(1, groups):
                got = dgrp.at[partner(k)]
                copy(got, got, dg_s.at[k], dg_r.at[k], row=sibling).wait_recv()
        scatter_start(phase)
        if phase + 1 < phases:
            for n in range(early):
                pass_on(phase + 1, n)
        if phase:
            scatter_finish(phase - 1)
        if phase >= 3:
            drain(phase - 3)
    deliver(before_ref, lambda q, p: bufs[STEPS - 1][q, r, part(q, p), :])
    scatter_finish(phases - 1)
    deliver(last_ref, lambda q, p: stage[(STEPS - 1) * CHUNKS + q, g, part(q, p), :])
    for phase in range(phases - 3, phases):
        drain(phase)


def per_device(t_start, h_blocks, h_cols, t_cols):
    groups, rows = lax.axis_size("grp"), lax.axis_size("row")
    rb, cb = t_start.shape[0] // BS, t_start.shape[1] // BS
    hrows, slots = h_blocks.shape[0], h_blocks.shape[2]
    keeps = t_cols.shape[1]
    nblk = rows * rb
    pairs = rows // 2
    wide = rb * BS
    dense = hrows * nblk * BS * BS * 2 <= DENSE_BYTES
    phases = STEPS * CHUNKS
    dma = pltpu.SemaphoreType.DMA
    out = pltpu.VMEM(t_start.shape, t_start.dtype)
    return pl.pallas_call(
        functools.partial(kernel, (groups, rows, rb, cb, keeps, hrows, slots, dense)),
        out_shape=(out, out),
        in_specs=[
            pl.BlockSpec(memory_space=pl.ANY),
            pl.BlockSpec(memory_space=pl.ANY),
            pl.BlockSpec(memory_space=pl.ANY),
            pl.BlockSpec(memory_space=pl.ANY),
        ],
        out_specs=(pl.BlockSpec(memory_space=pltpu.VMEM),) * 2,
        scratch_shapes=[
            pltpu.VMEM((CHUNKS, rows, cb * WIDEST + TILE, wide), BF16),
            *[pltpu.VMEM((CHUNKS, rows, keeps * WIDEST, wide), BF16) for _ in range(STEPS - 1)],
            pltpu.VMEM(t_start.shape, BF16),
            pltpu.VMEM((hrows, slots, BS, BS), BF16),
            pltpu.VMEM((hrows, slots + 1, BS, BS), BF16),
            pltpu.VMEM((nblk, BS, hrows * BS) if dense else (1, TILE, BS), BF16),
            pltpu.VMEM((1, TILE, BS) if dense else (nblk, cb * WIDEST, BS), BF16),
            pltpu.VMEM((groups, cb * WIDEST, wide), F32),
            pltpu.VMEM((phases, groups, keeps * WIDEST, wide), BF16),
            pltpu.VMEM((phases, groups, keeps * WIDEST, wide), BF16),
            pltpu.VMEM((groups, TILE, wide), BF16),
            pltpu.SMEM(h_cols.shape, jnp.int32),
            pltpu.SMEM(t_cols.shape, jnp.int32),
            dma((phases, 4)),
            dma((phases, pairs)),
            dma((phases, pairs)),
            dma((phases, pairs)),
            dma((phases, pairs)),
            dma((phases, groups)),
            dma((phases, groups)),
            dma((groups,)),
            dma((groups,)),
            dma((4,)),
        ],
        compiler_params=pltpu.CompilerParams(
            collective_id=0, has_side_effects=True, vmem_limit_bytes=56 << 20
        ),
    )(t_start, h_blocks, h_cols, t_cols)


def solution(mesh):
    placed = (
        P(("row", "grp"), None),
        P("row", "grp", None, None, None),
        P("row", "grp", None),
        P(("row", "grp"), None),
    )
    return jax.shard_map(
        per_device,
        mesh=mesh,
        in_specs=placed,
        out_specs=(P(("row", "grp"), None), P(("row", "grp"), None)),
        check_vma=False,
    )
```

```python
import functools

import jax
import jax.numpy as jnp
from jax import lax
from jax.experimental import pallas as pl
from jax.experimental.pallas import tpu as pltpu
from jax.sharding import PartitionSpec as P

BS = 128
STEPS = 3
SIZES = (32, 32, 32, 32)
CHUNKS = len(SIZES)
FROM = tuple(sum(SIZES[:q]) for q in range(CHUNKS))
WIDEST = max(SIZES)
TILE = 16
MESH = pl.DeviceIdType.MESH
BF16 = jnp.bfloat16
F32 = jnp.float32
DENSE_BYTES = 8 << 20
AHEAD = 3


def kernel(dims, t_hbm, h_hbm, hc_hbm, tc_hbm, before_ref, last_ref, *scratch):
    groups, rows, rb, cb, keeps, hrows, slots, dense = dims
    bufs = scratch[:STEPS]
    tv, hs, hst, hd, unp, acc, stage, landed, dgrp, hc, tc = scratch[STEPS : STEPS + 11]
    ag_s, rl_s, rs_s, rs_r, ag_r, fw_r, dg_s, dg_r, local = scratch[STEPS + 11 :]
    pairs = rows // 2
    nblk = rows * rb
    full = [cb * size for size in SIZES]
    packed = [keeps * size for size in SIZES]
    wide = rb * BS
    phases = STEPS * CHUNKS
    g = lax.axis_index("grp")
    r = lax.axis_index("row")
    pair, core = r // 2, lax.rem(r, 2)
    sibling = pair * 2 + 1 - core

    def part(q, c):
        return slice(c * SIZES[q], (c + 1) * SIZES[q])

    def copy(src, dst, ss, rs, row=None, grp=None):
        return pltpu.make_async_remote_copy(
            src_ref=src,
            dst_ref=dst,
            send_sem=ss,
            recv_sem=rs,
            device_id=(g if grp is None else grp, r if row is None else row),
            device_id_type=MESH,
        )

    t_copy = pltpu.make_async_copy(t_hbm, tv, local.at[0])
    t_copy.start()
    tc_copy = pltpu.make_async_copy(tc_hbm, tc, local.at[1])
    tc_copy.start()
    reach = [d for d in (2, -2, 1, -1) if abs(d) < pairs]

    def inside(d):
        return (pair + d >= 0) & (pair + d < pairs)

    def partner(k):
        other = g
        for i in range(groups.bit_length() - 1):
            if k >> i & 1:
                other = other + (1 - 2 * lax.rem(g // (1 << i), 2)) * (1 << i)
        return other

    def there(d):
        if abs(d) == 1:
            return inside(d)
        return (pair + d > 0) & (pair + d < pairs - 1)

    def at_pair(d):
        return lax.rem(pair + d + 2 * pairs, pairs) * 2 + core

    barrier = pltpu.get_barrier_semaphore()
    greeted = jnp.int32(groups)
    for k in range(1, groups):
        pl.semaphore_signal(barrier, inc=1, device_id=(partner(k), r), device_id_type=MESH)
    pl.semaphore_signal(barrier, inc=1, device_id=(g, sibling), device_id_type=MESH)
    for d in reach:

        @pl.when(inside(d))
        def _():
            pl.semaphore_signal(barrier, inc=1, device_id=(g, at_pair(d)), device_id_type=MESH)

        greeted = greeted + jnp.where(inside(d), 1, 0)

    h_copy = pltpu.make_async_copy(h_hbm.at[:, 0], hs, local.at[2])
    h_copy.start()
    hc_copy = pltpu.make_async_copy(hc_hbm, hc, local.at[3])
    hc_copy.start()
    tc_copy.wait()
    lanes = []
    for b in range(rb):
        total = tc[b, 0]
        for s in range(1, keeps):
            total = total + tc[b, s]
        lanes.append(jnp.full((TILE, BS), cb * (cb - 1) // 2 - total, jnp.int32).astype(F32).astype(BF16))
    mark = jnp.concatenate(lanes, axis=1)
    dgrp[g] = mark
    bufs[0][0, r, full[0] : full[0] + TILE, :] = mark
    t_copy.wait()
    turned = tv[...].T
    for q in range(CHUNKS):
        for c in range(cb):
            at = c * BS + FROM[q]
            bufs[0][q, r, part(q, c), :] = turned[at : at + SIZES[q], :]
    pl.semaphore_wait(barrier, greeted)

    def go(one, cond=None):
        if cond is None:
            one.start()
        else:
            pl.when(cond)(one.start)

    def piece(phase, who):
        step, q = divmod(phase, CHUNKS)
        if step:
            return bufs[step].at[q, who, pl.ds(0, packed[q])]
        return bufs[0].at[q, who, pl.ds(0, full[q] + (0 if q else TILE))]

    def gather_start(phase):
        own = piece(phase, r)
        for d in reach:
            go(copy(own, own, ag_s.at[phase], ag_r.at[phase, pair], row=at_pair(d)), there(d))
        go(copy(own, own, ag_s.at[phase], fw_r.at[phase, pair], row=sibling))

    def ranked(p):
        far = 1 if 2 * p < pairs else -1
        short = lambda s: pairs == 4 and (s - p) * far < 0
        return sorted((s for s in range(pairs) if s != p), key=lambda s: (short(s), abs(s - p), (s - p) * far < 0))

    def kth(n):
        src = jnp.int32(ranked(0)[n])
        for p in range(1, pairs):
            src = jnp.where(pair == p, ranked(p)[n], src)
        toward = jnp.where(src > pair, 1, -1)
        return src, (src - pair) * toward, toward

    order = [kth(n) for n in range(pairs - 1)]

    for k in range(1, groups):
        go(copy(dgrp.at[g], dgrp.at[g], dg_s.at[k], dg_r.at[k], grp=partner(k)))
    for q in range(AHEAD):
        gather_start(q)

    def turn_blocks():
        h_copy.wait()
        hc_copy.wait()
        for b in range(hrows):
            turned = hs[b].reshape(slots * BS, BS).T
            for s in range(slots):
                hst[b, s] = turned[:, s * BS : (s + 1) * BS]
            if dense:
                hst[b, slots] = jnp.zeros((BS, BS), BF16)

    def lay_out():
        def build(c, carry):
            named = (c // rb) * (groups * rb) + g * rb + lax.rem(c, rb)
            for b in range(hrows):
                at = jnp.int32(slots)
                for s in range(slots):
                    at = jnp.where(hc[b, 0, s] == named, s, at)
                hd[c, :, b * BS : (b + 1) * BS] = hst[b, at]
            return carry

        lax.fori_loop(0, nblk, build, 0)

    def tall(q, tile):
        return jnp.concatenate([tile] * (SIZES[q] // TILE), axis=0)

    def gone_of(q, who):
        return tall(q, bufs[0][0, who, full[0] : full[0] + TILE, :])

    def unpacked(gone, value):
        zero = jnp.zeros(gone.shape, BF16)
        out = []
        for c in range(cb):
            if c == 0:
                one = value(0)
            elif c == cb - 1:
                one = value(c - 1)
            else:
                one = jnp.where(gone < c, value(c - 1), value(c))
            out.append(jnp.where(gone == c, zero, one))
        return jnp.concatenate(out, axis=0)

    def operand(phase, who):
        step, q = divmod(phase, CHUNKS)
        if step == 0:
            return bufs[0][q, who, : full[q], :]
        return unpacked(gone_of(q, who), lambda p: bufs[step][q, who, part(q, p), :])

    def multiply_half(phase, who, first):
        high = full[phase % CHUNKS]
        if not dense:
            one = operand(phase, who)
            for b in range(rb):
                unp[who * rb + b, :high] = one[:, b * BS : (b + 1) * BS]
            return
        right = hd[pl.ds(who * rb, rb)].reshape(wide, hrows * BS)
        out = jnp.dot(operand(phase, who), right, preferred_element_type=F32)
        for k in range(groups):
            value = out[:, k * wide : (k + 1) * wide]
            acc[k, :high] = value if first else acc[k, :high] + value

    def multiply(phase, src, first):
        both = [operand(phase, src * 2 + n) for n in range(2)]
        high = full[phase % CHUNKS]
        if not dense:
            for n in range(2):
                for b in range(rb):
                    unp[(src * 2 + n) * rb + b, :high] = both[n][:, b * BS : (b + 1) * BS]
            return
        right = hd[pl.ds(src * 2 * rb, 2 * rb)].reshape(2 * wide, hrows * BS)
        out = jnp.dot(jnp.concatenate(both, axis=1), right, preferred_element_type=F32)
        for k in range(groups):
            value = out[:, k * wide : (k + 1) * wide]
            acc[k, :high] = value if first else acc[k, :high] + value

    def multiply_sparse(phase):
        high = full[phase % CHUNKS]

        def one_group(k, carry):
            for b in range(rb):
                i = k * rb + b
                out = jnp.zeros((high, BS), F32)
                for s in range(slots):
                    named = hc[i, 0, s]
                    at = named // (groups * rb) * rb + lax.rem(named, rb)
                    out = out + jnp.dot(unp[at][:high], hst[i, s], preferred_element_type=F32)
                acc[k, :high, b * BS : (b + 1) * BS] = out
            return carry

        lax.fori_loop(0, groups, one_group, 0)

    def forwarded(phase, src):
        got = piece(phase, src * 2 + 1 - core)
        copy(got, got, ag_s.at[phase], fw_r.at[phase, src], row=sibling).wait_recv()

    def relayed(src, apart, toward):
        beyond = pair - toward
        return ((apart >= 2) | (beyond == 0) | (beyond == pairs - 1)) & (beyond >= 0) & (beyond < pairs)

    def total(conds):
        return sum(jnp.where(cond, 1, 0) for cond in conds)

    sent = total(there(d) for d in reach) + pairs
    passed = total(relayed(*one) for one in order)

    def drain(phase):
        step, q = divmod(phase, CHUNKS)
        high = packed[q] if step else full[q] + (0 if q else TILE)

        def settle(sem, count, choices):
            for n in choices:

                @pl.when(count == n)
                def _():
                    some = bufs[step].at[q, pl.ds(0, n), pl.ds(0, high)]
                    copy(some, some, sem.at[phase], sem.at[phase], row=sibling).wait_send()

        few = pairs == 4
        settle(ag_s, sent, [pairs + 2] if few else range(pairs, pairs + 5))
        settle(rl_s, passed, [2] if few else range(1, pairs))
        some = stage.at[phase, pl.ds(0, groups - 1), pl.ds(0, packed[q])]
        copy(some, some, rs_s.at[phase], rs_s.at[phase], row=sibling).wait_send()

    def pass_on(phase, n):
        src, apart, toward = order[n]
        got = piece(phase, src * 2 + core)
        copy(got, got, ag_s.at[phase], ag_r.at[phase, src], row=sibling).wait_recv()
        beyond = pair - toward
        go(
            copy(got, got, rl_s.at[phase], ag_r.at[phase, src], row=lax.rem(beyond + pairs, pairs) * 2 + core),
            relayed(src, apart, toward),
        )
        go(copy(got, got, ag_s.at[phase], fw_r.at[phase, src], row=sibling))

    def gather_multiply(phase, done):
        before = pair
        for n, (src, _, _) in enumerate(order):
            if n >= done:
                pass_on(phase, n)
            forwarded(phase, before)
            multiply(phase, before, n == 0)
            before = src
        multiply_half(phase, before * 2 + core, pairs == 1)
        forwarded(phase, before)
        multiply_half(phase, before * 2 + 1 - core, False)
        if not dense:
            multiply_sparse(phase)

    def scatter_start(phase):
        q = phase % CHUNKS
        rows_here = pl.ds(0, packed[q])
        for k in [*range(groups - 1, 0, -1), 0]:
            to = partner(k)
            gone = tall(q, dgrp[to])
            for p in range(keeps):
                low, high = acc[to, part(q, p), :].astype(BF16), acc[to, part(q, p + 1), :].astype(BF16)
                stage[phase, to, part(q, p), :] = jnp.where(gone > p, low, high)
            if k:
                go(copy(stage.at[phase, to, rows_here], landed.at[phase, g, rows_here], rs_s.at[phase], rs_r.at[phase], grp=to))

    def scatter_finish(phase):
        step, q = divmod(phase, CHUNKS)
        got = landed.at[phase, pl.ds(0, groups - 1), pl.ds(0, packed[q])]
        copy(got, got, rs_s.at[phase], rs_r.at[phase], row=sibling).wait_recv()
        gone = tall(q, dgrp[g])
        for p in range(keeps):
            new = stage[phase, g, part(q, p), :].astype(F32)
            for k in range(1, groups):
                new = new + landed[phase, partner(k), part(q, p), :].astype(F32)
            if step == 1:
                old = jnp.where(gone > p, bufs[0][q, r, part(q, p), :], bufs[0][q, r, part(q, p + 1), :])
                new = 2.0 * new - old.astype(F32)
            elif step > 1:
                new = 2.0 * new - bufs[step - 1][q, r, part(q, p), :].astype(F32)
            if step < STEPS - 1:
                bufs[step + 1][q, r, part(q, p), :] = new.astype(BF16)
            else:
                stage[phase, g, part(q, p), :] = new.astype(BF16)
        if step < STEPS - 1:
            gather_start(phase + CHUNKS)

    def deliver(ref, source):
        pieces = [unpacked(tall(q, dgrp[g]), functools.partial(source, q)) for q in range(CHUNKS)]
        whole = jnp.concatenate([pieces[q][part(q, c), :] for c in range(cb) for q in range(CHUNKS)], axis=0)
        ref[...] = whole.T

    turn_blocks()
    early = min(2, len(order))
    for n in range(early):
        pass_on(0, n)
    for q in range(AHEAD, CHUNKS):
        gather_start(q)
    if dense:
        lay_out()
    for phase in range(phases):
        gather_multiply(phase, early)
        if phase == 0:
            for k in range(1, groups):
                got = dgrp.at[partner(k)]
                copy(got, got, dg_s.at[k], dg_r.at[k], row=sibling).wait_recv()
        scatter_start(phase)
        if phase + 1 < phases:
            for n in range(early):
                pass_on(phase + 1, n)
        if phase:
            scatter_finish(phase - 1)
        if phase >= 3:
            drain(phase - 3)
    deliver(before_ref, lambda q, p: bufs[STEPS - 1][q, r, part(q, p), :])
    scatter_finish(phases - 1)
    deliver(last_ref, lambda q, p: stage[(STEPS - 1) * CHUNKS + q, g, part(q, p), :])
    for phase in range(phases - 3, phases):
        drain(phase)
    for k in range(1, groups):
        copy(dgrp.at[g], dgrp.at[g], dg_s.at[k], dg_r.at[k], row=sibling).wait_send()


def per_device(t_start, h_blocks, h_cols, t_cols):
    groups, rows = lax.axis_size("grp"), lax.axis_size("row")
    rb, cb = t_start.shape[0] // BS, t_start.shape[1] // BS
    hrows, slots = h_blocks.shape[0], h_blocks.shape[2]
    keeps = t_cols.shape[1]
    nblk = rows * rb
    pairs = rows // 2
    wide = rb * BS
    dense = hrows * nblk * BS * BS * 2 <= DENSE_BYTES
    phases = STEPS * CHUNKS
    dma = pltpu.SemaphoreType.DMA
    out = pltpu.VMEM(t_start.shape, t_start.dtype)
    return pl.pallas_call(
        functools.partial(kernel, (groups, rows, rb, cb, keeps, hrows, slots, dense)),
        out_shape=(out, out),
        in_specs=[
            pl.BlockSpec(memory_space=pl.ANY),
            pl.BlockSpec(memory_space=pl.ANY),
            pl.BlockSpec(memory_space=pl.ANY),
            pl.BlockSpec(memory_space=pl.ANY),
        ],
        out_specs=(pl.BlockSpec(memory_space=pltpu.VMEM),) * 2,
        scratch_shapes=[
            pltpu.VMEM((CHUNKS, rows, cb * WIDEST + TILE, wide), BF16),
            *[pltpu.VMEM((CHUNKS, rows, keeps * WIDEST, wide), BF16) for _ in range(STEPS - 1)],
            pltpu.VMEM(t_start.shape, BF16),
            pltpu.VMEM((hrows, slots, BS, BS), BF16),
            pltpu.VMEM((hrows, slots + 1, BS, BS), BF16),
            pltpu.VMEM((nblk, BS, hrows * BS) if dense else (1, TILE, BS), BF16),
            pltpu.VMEM((1, TILE, BS) if dense else (nblk, cb * WIDEST, BS), BF16),
            pltpu.VMEM((groups, cb * WIDEST, wide), F32),
            pltpu.VMEM((phases, groups, keeps * WIDEST, wide), BF16),
            pltpu.VMEM((phases, groups, keeps * WIDEST, wide), BF16),
            pltpu.VMEM((groups, TILE, wide), BF16),
            pltpu.SMEM(h_cols.shape, jnp.int32),
            pltpu.SMEM(t_cols.shape, jnp.int32),
            dma((phases,)),
            dma((phases,)),
            dma((phases,)),
            dma((phases,)),
            dma((phases, pairs)),
            dma((phases, pairs)),
            dma((groups,)),
            dma((groups,)),
            dma((4,)),
        ],
        compiler_params=pltpu.CompilerParams(
            collective_id=0, has_side_effects=True, vmem_limit_bytes=56 << 20
        ),
    )(t_start, h_blocks, h_cols, t_cols)


def solution(mesh):
    placed = (
        P(("row", "grp"), None),
        P("row", "grp", None, None, None),
        P("row", "grp", None),
        P(("row", "grp"), None),
    )
    return jax.shard_map(
        per_device,
        mesh=mesh,
        in_specs=placed,
        out_specs=(P(("row", "grp"), None), P(("row", "grp"), None)),
        check_vma=False,
    )
```

```python
import functools

import jax
import jax.numpy as jnp
from jax import lax
from jax.experimental import pallas as pl
from jax.experimental.pallas import tpu as pltpu
from jax.sharding import PartitionSpec as P

BS = 128
STEPS = 3
SIZES = (32, 32, 32, 32)
CHUNKS = len(SIZES)
FROM = tuple(sum(SIZES[:q]) for q in range(CHUNKS))
WIDEST = max(SIZES)
TILE = 16
MESH = pl.DeviceIdType.MESH
BF16 = jnp.bfloat16
F32 = jnp.float32
DENSE_BYTES = 8 << 20
AHEAD = 3


def kernel(dims, t_hbm, h_hbm, hc_hbm, tc_hbm, before_ref, last_ref, *scratch):
    groups, rows, rb, cb, keeps, hrows, slots, dense = dims
    bufs = scratch[:STEPS]
    tv, hs, hst, hd, unp, acc, stage, landed, dgrp, hc, tc = scratch[STEPS : STEPS + 11]
    ag_s, rl_s, rs_s, rs_r, ag_r, fw_r, dg_s, dg_r, local = scratch[STEPS + 11 :]
    pairs = rows // 2
    nblk = rows * rb
    full = [cb * size for size in SIZES]
    packed = [keeps * size for size in SIZES]
    wide = rb * BS
    phases = STEPS * CHUNKS
    g = lax.axis_index("grp")
    r = lax.axis_index("row")
    pair, core = r // 2, lax.rem(r, 2)
    sibling = pair * 2 + 1 - core
    home = core * pairs + pair

    def part(q, c):
        return slice(c * SIZES[q], (c + 1) * SIZES[q])

    def copy(src, dst, ss, rs, row=None, grp=None):
        return pltpu.make_async_remote_copy(
            src_ref=src,
            dst_ref=dst,
            send_sem=ss,
            recv_sem=rs,
            device_id=(g if grp is None else grp, r if row is None else row),
            device_id_type=MESH,
        )

    t_copy = pltpu.make_async_copy(t_hbm, tv, local.at[0])
    t_copy.start()
    tc_copy = pltpu.make_async_copy(tc_hbm, tc, local.at[1])
    tc_copy.start()
    reach = [d for d in (2, -2, 1, -1) if abs(d) < pairs]

    def inside(d):
        return (pair + d >= 0) & (pair + d < pairs)

    def partner(k):
        other = g
        for i in range(groups.bit_length() - 1):
            if k >> i & 1:
                other = other + (1 - 2 * lax.rem(g // (1 << i), 2)) * (1 << i)
        return other

    def goals(p):
        return [p + d for d in reach if (0 <= p + d < pairs if abs(d) == 1 else 0 < p + d < pairs - 1)]

    def pick(values):
        out = jnp.int32(values[0])
        if len(set(values)) > 1:
            for p in range(1, pairs):
                out = jnp.where(pair == p, values[p], out)
        return out

    def at_pair(d):
        return lax.rem(pair + d + 2 * pairs, pairs) * 2 + core

    barrier = pltpu.get_barrier_semaphore()
    greeted = jnp.int32(groups)
    for k in range(1, groups):
        pl.semaphore_signal(barrier, inc=1, device_id=(partner(k), r), device_id_type=MESH)
    pl.semaphore_signal(barrier, inc=1, device_id=(g, sibling), device_id_type=MESH)
    for d in reach:

        @pl.when(inside(d))
        def _():
            pl.semaphore_signal(barrier, inc=1, device_id=(g, at_pair(d)), device_id_type=MESH)

        greeted = greeted + jnp.where(inside(d), 1, 0)

    h_copy = pltpu.make_async_copy(h_hbm.at[:, 0], hs, local.at[2])
    h_copy.start()
    hc_copy = pltpu.make_async_copy(hc_hbm, hc, local.at[3])
    hc_copy.start()
    tc_copy.wait()
    lanes = []
    for b in range(rb):
        total = tc[b, 0]
        for s in range(1, keeps):
            total = total + tc[b, s]
        lanes.append(jnp.full((TILE, BS), cb * (cb - 1) // 2 - total, jnp.int32).astype(F32).astype(BF16))
    mark = jnp.concatenate(lanes, axis=1)
    dgrp[g] = mark
    bufs[0][0, home, full[0] : full[0] + TILE, :] = mark
    t_copy.wait()
    turned = tv[...].T
    for q in range(CHUNKS):
        for c in range(cb):
            at = c * BS + FROM[q]
            bufs[0][q, home, part(q, c), :] = turned[at : at + SIZES[q], :]
    pl.semaphore_wait(barrier, greeted)

    def go(one, cond=None):
        if cond is None:
            one.start()
        else:
            pl.when(cond)(one.start)

    def piece(phase, who):
        step, q = divmod(phase, CHUNKS)
        if step:
            return bufs[step].at[q, who, pl.ds(0, packed[q])]
        return bufs[0].at[q, who, pl.ds(0, full[q] + (0 if q else TILE))]

    def ranked(p):
        far = 1 if 2 * p < pairs else -1
        short = lambda s: pairs == 4 and (s - p) * far < 0
        return sorted((s for s in range(pairs) if s != p), key=lambda s: (short(s), abs(s - p), (s - p) * far < 0))

    def beyond(p, n):
        src = ranked(p)[n]
        to = p + (1 if src < p else -1)
        return to if 0 <= to < pairs and to not in goals(src) else None

    def counted(lists, k):
        have = [int(len(one) > k) for one in lists]
        return None if all(have) else pick(have) == 1

    every = range(pairs)
    targets = [goals(p) for p in every]
    sent = [len(one) + pairs for one in targets]
    onward = [[beyond(p, n) for n in range(pairs - 1)] for p in every]
    passed = [sum(to is not None for to in one) for one in onward]
    order = [pick([ranked(p)[n] for p in every]) for n in range(pairs - 1)]
    early = 2

    def gather_start(phase):
        own = piece(phase, home)
        for k in range(max(len(one) for one in targets)):
            to = pick([one[k] if k < len(one) else one[0] for one in targets])
            go(copy(own, own, ag_s.at[phase], ag_r.at[phase, pair], row=to * 2 + core), counted(targets, k))
        go(copy(own, own, ag_s.at[phase], fw_r.at[phase, pair], row=sibling))

    for k in range(1, groups):
        go(copy(dgrp.at[g], dgrp.at[g], dg_s.at[k], dg_r.at[k], grp=partner(k)))
    for q in range(AHEAD):
        gather_start(q)

    def turn_blocks():
        h_copy.wait()
        hc_copy.wait()
        for b in range(hrows):
            turned = hs[b].reshape(slots * BS, BS).T
            for s in range(slots):
                hst[b, s] = turned[:, s * BS : (s + 1) * BS]
            if dense:
                hst[b, slots] = jnp.zeros((BS, BS), BF16)

    def lay_out():
        def build(c, carry):
            named = (c // rb) * (groups * rb) + g * rb + lax.rem(c, rb)
            for b in range(hrows):
                at = jnp.int32(slots)
                for s in range(slots):
                    at = jnp.where(hc[b, 0, s] == named, s, at)
                hd[c, :, b * BS : (b + 1) * BS] = hst[b, at]
            return carry

        lax.fori_loop(0, nblk, build, 0)

    def tall(q, tile):
        return jnp.concatenate([tile] * (SIZES[q] // TILE), axis=0)

    def gone_of(q, who):
        return tall(q, bufs[0][0, who, full[0] : full[0] + TILE, :])

    def unpacked(gone, value):
        zero = jnp.zeros(gone.shape, BF16)
        out = []
        for c in range(cb):
            if c == 0:
                one = value(0)
            elif c == cb - 1:
                one = value(c - 1)
            else:
                one = jnp.where(gone < c, value(c - 1), value(c))
            out.append(jnp.where(gone == c, zero, one))
        return jnp.concatenate(out, axis=0)

    def operand(phase, who):
        step, q = divmod(phase, CHUNKS)
        if step == 0:
            return bufs[0][q, who, : full[q], :]
        return unpacked(gone_of(q, who), lambda p: bufs[step][q, who, part(q, p), :])

    def keep_apart(value, src, n):
        for b in range(rb):
            unp[(src * 2 + n) * rb + b, : value.shape[0]] = value[:, b * BS : (b + 1) * BS]

    def accumulate(phase, left, right, first):
        high = full[phase % CHUNKS]
        out = jnp.dot(left, right.reshape(left.shape[1], hrows * BS), preferred_element_type=F32)
        for k in range(groups):
            value = out[:, k * wide : (k + 1) * wide]
            acc[k, :high] = value if first else acc[k, :high] + value

    def multiply_half(phase, src, n):
        one = operand(phase, n * pairs + src)
        if dense:
            accumulate(phase, one, hd[pl.ds((src * 2 + n) * rb, rb)], False)
        else:
            keep_apart(one, src, n)

    def multiply(phase, src, first):
        both = [operand(phase, n * pairs + src) for n in range(2)]
        if dense:
            accumulate(phase, jnp.concatenate(both, axis=1), hd[pl.ds(src * 2 * rb, 2 * rb)], first)
        else:
            for n in range(2):
                keep_apart(both[n], src, n)

    def multiply_sparse(phase):
        high = full[phase % CHUNKS]

        def one_group(k, carry):
            for b in range(rb):
                i = k * rb + b
                out = jnp.zeros((high, BS), F32)
                for s in range(slots):
                    named = hc[i, 0, s]
                    at = named // (groups * rb) * rb + lax.rem(named, rb)
                    out = out + jnp.dot(unp[at][:high], hst[i, s], preferred_element_type=F32)
                acc[k, :high, b * BS : (b + 1) * BS] = out
            return carry

        lax.fori_loop(0, groups, one_group, 0)

    def forwarded(phase, src):
        got = piece(phase, (1 - core) * pairs + src)
        copy(got, got, ag_s.at[phase], fw_r.at[phase, src], row=sibling).wait_recv()

    def drain(phase):
        step, q = divmod(phase, CHUNKS)
        high = packed[q] if step else full[q] + (0 if q else TILE)

        def settle(sem, counts):
            for n in sorted(set(counts) - {0}):

                def wait():
                    some = bufs[step].at[q, pl.ds(0, n), pl.ds(0, high)]
                    copy(some, some, sem.at[phase], sem.at[phase], row=sibling).wait_send()

                if len(set(counts)) == 1:
                    wait()
                else:
                    pl.when(pick(counts) == n)(wait)

        settle(ag_s, sent)
        settle(rl_s, passed)
        some = stage.at[phase, pl.ds(0, groups - 1), pl.ds(0, packed[q])]
        copy(some, some, rs_s.at[phase], rs_s.at[phase], row=sibling).wait_send()

    def pass_on(phase, n):
        src = order[n]
        got = piece(phase, core * pairs + src)
        copy(got, got, ag_s.at[phase], ag_r.at[phase, src], row=sibling).wait_recv()
        tos = [one[n] for one in onward]
        if any(to is not None for to in tos):
            to = pick([p if to is None else to for p, to in enumerate(tos)])
            go(
                copy(got, got, rl_s.at[phase], ag_r.at[phase, src], row=to * 2 + core),
                None if None not in tos else pick([int(one is not None) for one in tos]) == 1,
            )
        go(copy(got, got, ag_s.at[phase], fw_r.at[phase, src], row=sibling))

    def gather_multiply(phase):
        forwarded(phase, pair)
        multiply(phase, pair, True)
        last = len(order) - 1
        for n, src in enumerate(order):
            if n >= early - 1 and n < last:
                pass_on(phase, n + 1)
            if n < last:
                forwarded(phase, src)
                multiply(phase, src, False)
            else:
                multiply_half(phase, src, core)
                forwarded(phase, src)
                multiply_half(phase, src, 1 - core)
        if not dense:
            multiply_sparse(phase)

    def scatter_start(phase):
        q = phase % CHUNKS
        rows_here = pl.ds(0, packed[q])
        for k in [*range(groups - 1, 0, -1), 0]:
            to = partner(k)
            gone = tall(q, dgrp[to])
            for p in range(keeps):
                low, high = acc[to, part(q, p), :].astype(BF16), acc[to, part(q, p + 1), :].astype(BF16)
                stage[phase, to, part(q, p), :] = jnp.where(gone > p, low, high)
            if k:
                go(copy(stage.at[phase, to, rows_here], landed.at[phase, g, rows_here], rs_s.at[phase], rs_r.at[phase], grp=to))

    def scatter_finish(phase):
        step, q = divmod(phase, CHUNKS)
        got = landed.at[phase, pl.ds(0, groups - 1), pl.ds(0, packed[q])]
        copy(got, got, rs_s.at[phase], rs_r.at[phase], row=sibling).wait_recv()
        gone = tall(q, dgrp[g])
        for p in range(keeps):
            new = stage[phase, g, part(q, p), :].astype(F32)
            for k in range(1, groups):
                new = new + landed[phase, partner(k), part(q, p), :].astype(F32)
            if step == 1:
                old = jnp.where(gone > p, bufs[0][q, home, part(q, p), :], bufs[0][q, home, part(q, p + 1), :])
                new = 2.0 * new - old.astype(F32)
            elif step > 1:
                new = 2.0 * new - bufs[step - 1][q, home, part(q, p), :].astype(F32)
            if step < STEPS - 1:
                bufs[step + 1][q, home, part(q, p), :] = new.astype(BF16)
            else:
                stage[phase, g, part(q, p), :] = new.astype(BF16)
        if step < STEPS - 1:
            gather_start(phase + CHUNKS)

    def deliver(ref, source):
        pieces = [unpacked(tall(q, dgrp[g]), functools.partial(source, q)) for q in range(CHUNKS)]
        whole = jnp.concatenate([pieces[q][part(q, c), :] for c in range(cb) for q in range(CHUNKS)], axis=0)
        ref[...] = whole.T

    def first_part(phase):
        for n in range(early):
            pass_on(phase, n)

    turn_blocks()
    first_part(0)
    for q in range(AHEAD, CHUNKS):
        gather_start(q)
    if dense:
        lay_out()
    for phase in range(phases):
        gather_multiply(phase)
        if phase == 0:
            for k in range(1, groups):
                got = dgrp.at[partner(k)]
                copy(got, got, dg_s.at[k], dg_r.at[k], row=sibling).wait_recv()
        scatter_start(phase)
        if phase + 1 < phases:
            first_part(phase + 1)
        if phase:
            scatter_finish(phase - 1)
        if phase >= 3:
            drain(phase - 3)
    deliver(before_ref, lambda q, p: bufs[STEPS - 1][q, home, part(q, p), :])
    scatter_finish(phases - 1)
    deliver(last_ref, lambda q, p: stage[(STEPS - 1) * CHUNKS + q, g, part(q, p), :])
    for phase in range(phases - 3, phases):
        drain(phase)
    for k in range(1, groups):
        copy(dgrp.at[g], dgrp.at[g], dg_s.at[k], dg_r.at[k], row=sibling).wait_send()


def hand_out(before, last, before_hbm, last_hbm, sems):
    copies = [
        pltpu.make_async_copy(before, before_hbm, sems.at[0]),
        pltpu.make_async_copy(last, last_hbm, sems.at[1]),
    ]
    for one in copies:
        one.start()
    for one in copies:
        one.wait()


def per_device(t_start, h_blocks, h_cols, t_cols):
    groups, rows = lax.axis_size("grp"), lax.axis_size("row")
    rb, cb = t_start.shape[0] // BS, t_start.shape[1] // BS
    hrows, slots = h_blocks.shape[0], h_blocks.shape[2]
    keeps = t_cols.shape[1]
    nblk = rows * rb
    pairs = rows // 2
    wide = rb * BS
    dense = hrows * nblk * BS * BS * 2 <= DENSE_BYTES
    phases = STEPS * CHUNKS
    dma = pltpu.SemaphoreType.DMA
    out = pltpu.VMEM(t_start.shape, t_start.dtype)
    held = pl.pallas_call(
        functools.partial(kernel, (groups, rows, rb, cb, keeps, hrows, slots, dense)),
        out_shape=(out, out),
        in_specs=[
            pl.BlockSpec(memory_space=pl.ANY),
            pl.BlockSpec(memory_space=pl.ANY),
            pl.BlockSpec(memory_space=pl.ANY),
            pl.BlockSpec(memory_space=pl.ANY),
        ],
        out_specs=(pl.BlockSpec(memory_space=pltpu.VMEM),) * 2,
        scratch_shapes=[
            pltpu.VMEM((CHUNKS, rows, cb * WIDEST + TILE, wide), BF16),
            *[pltpu.VMEM((CHUNKS, rows, keeps * WIDEST, wide), BF16) for _ in range(STEPS - 1)],
            pltpu.VMEM(t_start.shape, BF16),
            pltpu.VMEM((hrows, slots, BS, BS), BF16),
            pltpu.VMEM((hrows, slots + 1, BS, BS), BF16),
            pltpu.VMEM((nblk, BS, hrows * BS) if dense else (1, TILE, BS), BF16),
            pltpu.VMEM((1, TILE, BS) if dense else (nblk, cb * WIDEST, BS), BF16),
            pltpu.VMEM((groups, cb * WIDEST, wide), F32),
            pltpu.VMEM((phases, groups, keeps * WIDEST, wide), BF16),
            pltpu.VMEM((phases, groups, keeps * WIDEST, wide), BF16),
            pltpu.VMEM((groups, TILE, wide), BF16),
            pltpu.SMEM(h_cols.shape, jnp.int32),
            pltpu.SMEM(t_cols.shape, jnp.int32),
            dma((phases,)),
            dma((phases,)),
            dma((phases,)),
            dma((phases,)),
            dma((phases, pairs)),
            dma((phases, pairs)),
            dma((groups,)),
            dma((groups,)),
            dma((4,)),
        ],
        compiler_params=pltpu.CompilerParams(
            collective_id=0, has_side_effects=True, vmem_limit_bytes=56 << 20
        ),
    )(t_start, h_blocks, h_cols, t_cols)
    out = jax.ShapeDtypeStruct(t_start.shape, t_start.dtype)
    return pl.pallas_call(
        hand_out,
        out_shape=(out, out),
        in_specs=[pl.BlockSpec(memory_space=pltpu.VMEM)] * 2,
        out_specs=(pl.BlockSpec(memory_space=pl.ANY),) * 2,
        scratch_shapes=[dma((2,))],
        name="hand_out",
    )(*[pltpu.with_memory_space_constraint(one, pltpu.VMEM) for one in held])


def solution(mesh):
    placed = (
        P(("row", "grp"), None),
        P("row", "grp", None, None, None),
        P("row", "grp", None),
        P(("row", "grp"), None),
    )
    return jax.shard_map(
        per_device,
        mesh=mesh,
        in_specs=placed,
        out_specs=(P(("row", "grp"), None), P(("row", "grp"), None)),
        check_vma=False,
    )
```

```python
import functools

import jax
import jax.numpy as jnp
from jax import lax
from jax.experimental import pallas as pl
from jax.experimental.pallas import tpu as pltpu
from jax.sharding import PartitionSpec as P

BS = 128
STEPS = 3
SIZES = (32, 32, 32, 32)
CHUNKS = len(SIZES)
FROM = tuple(sum(SIZES[:q]) for q in range(CHUNKS))
WIDEST = max(SIZES)
TILE = 16
MESH = pl.DeviceIdType.MESH
BF16 = jnp.bfloat16
F32 = jnp.float32
DENSE_BYTES = 8 << 20
AHEAD = 3


def kernel(dims, t_hbm, h_hbm, hc_hbm, tc_hbm, before_ref, last_ref, *scratch):
    groups, rows, rb, cb, keeps, hrows, slots, dense = dims
    bufs = scratch[:STEPS]
    tv, hs, hst, hd, unp, acc, stage, landed, dgrp, hc, tc = scratch[STEPS : STEPS + 11]
    ag_s, rl_s, rs_s, rs_r, ag_r, fw_r, dg_s, dg_r, local = scratch[STEPS + 11 :]
    pairs = rows // 2
    nblk = rows * rb
    full = [cb * size for size in SIZES]
    packed = [keeps * size for size in SIZES]
    wide = rb * BS
    phases = STEPS * CHUNKS
    g = lax.axis_index("grp")
    r = lax.axis_index("row")
    pair, core = r // 2, lax.rem(r, 2)
    sibling = pair * 2 + 1 - core
    home = core * pairs + pair

    def part(q, c):
        return slice(c * SIZES[q], (c + 1) * SIZES[q])

    def copy(src, dst, ss, rs, row=None, grp=None):
        return pltpu.make_async_remote_copy(
            src_ref=src,
            dst_ref=dst,
            send_sem=ss,
            recv_sem=rs,
            device_id=(g if grp is None else grp, r if row is None else row),
            device_id_type=MESH,
        )

    t_copy = pltpu.make_async_copy(t_hbm, tv, local.at[0])
    t_copy.start()
    tc_copy = pltpu.make_async_copy(tc_hbm, tc, local.at[1])
    tc_copy.start()
    reach = [d for d in (2, -2, 1, -1) if abs(d) < pairs]

    def inside(d):
        return (pair + d >= 0) & (pair + d < pairs)

    def partner(k):
        other = g
        for i in range(groups.bit_length() - 1):
            if k >> i & 1:
                other = other + (1 - 2 * lax.rem(g // (1 << i), 2)) * (1 << i)
        return other

    def goals(p):
        return [p + d for d in reach if (0 <= p + d < pairs if abs(d) == 1 else 0 < p + d < pairs - 1)]

    def pick(values):
        out = jnp.int32(values[0])
        if len(set(values)) > 1:
            for p in range(1, pairs):
                out = jnp.where(pair == p, values[p], out)
        return out

    def at_pair(d):
        return lax.rem(pair + d + 2 * pairs, pairs) * 2 + core

    barrier = pltpu.get_barrier_semaphore()
    greeted = jnp.int32(groups)
    for k in range(1, groups):
        pl.semaphore_signal(barrier, inc=1, device_id=(partner(k), r), device_id_type=MESH)
    pl.semaphore_signal(barrier, inc=1, device_id=(g, sibling), device_id_type=MESH)
    for d in reach:

        @pl.when(inside(d))
        def _():
            pl.semaphore_signal(barrier, inc=1, device_id=(g, at_pair(d)), device_id_type=MESH)

        greeted = greeted + jnp.where(inside(d), 1, 0)

    h_copy = pltpu.make_async_copy(h_hbm.at[:, 0], hs, local.at[2])
    h_copy.start()
    hc_copy = pltpu.make_async_copy(hc_hbm, hc, local.at[3])
    hc_copy.start()
    tc_copy.wait()
    lanes = []
    for b in range(rb):
        total = tc[b, 0]
        for s in range(1, keeps):
            total = total + tc[b, s]
        lanes.append(jnp.full((TILE, BS), cb * (cb - 1) // 2 - total, jnp.int32).astype(F32).astype(BF16))
    mark = jnp.concatenate(lanes, axis=1)
    dgrp[g] = mark
    bufs[0][CHUNKS - 1, home, full[-1] : full[-1] + TILE, :] = mark
    t_copy.wait()
    turned = tv[...].T
    for q in range(CHUNKS):
        for c in range(cb):
            at = c * BS + FROM[q]
            bufs[0][q, home, part(q, c), :] = turned[at : at + SIZES[q], :]
    pl.semaphore_wait(barrier, greeted)

    def go(one, cond=None):
        if cond is None:
            one.start()
        else:
            pl.when(cond)(one.start)

    def piece(phase, who):
        step, q = divmod(phase, CHUNKS)
        if step:
            return bufs[step].at[q, who, pl.ds(0, packed[q])]
        return bufs[0].at[q, who, pl.ds(0, full[q] + (TILE if q == CHUNKS - 1 else 0))]

    def ranked(p):
        far = 1 if 2 * p < pairs else -1
        short = lambda s: pairs == 4 and (s - p) * far < 0
        return sorted((s for s in range(pairs) if s != p), key=lambda s: (short(s), abs(s - p), (s - p) * far < 0))

    def beyond(p, n):
        src = ranked(p)[n]
        to = p + (1 if src < p else -1)
        return to if 0 <= to < pairs and to not in goals(src) else None

    def counted(lists, k):
        have = [int(len(one) > k) for one in lists]
        return None if all(have) else pick(have) == 1

    every = range(pairs)
    targets = [goals(p) for p in every]
    sent = [len(one) + pairs for one in targets]
    onward = [[beyond(p, n) for n in range(pairs - 1)] for p in every]
    passed = [sum(to is not None for to in one) for one in onward]
    order = [pick([ranked(p)[n] for p in every]) for n in range(pairs - 1)]
    early = 2

    def gather_start(phase):
        own = piece(phase, home)
        for k in range(max(len(one) for one in targets)):
            to = pick([one[k] if k < len(one) else one[0] for one in targets])
            go(copy(own, own, ag_s.at[phase], ag_r.at[phase, pair], row=to * 2 + core), counted(targets, k))
        go(copy(own, own, ag_s.at[phase], fw_r.at[phase, pair], row=sibling))

    for k in range(1, groups):
        go(copy(dgrp.at[g], dgrp.at[g], dg_s.at[k], dg_r.at[k], grp=partner(k)))
    for q in range(AHEAD):
        gather_start(q)

    def turn_blocks():
        h_copy.wait()
        hc_copy.wait()
        for b in range(hrows):
            turned = hs[b].reshape(slots * BS, BS).T
            for s in range(slots):
                hst[b, s] = turned[:, s * BS : (s + 1) * BS]
            if dense:
                hst[b, slots] = jnp.zeros((BS, BS), BF16)

    def lay_out():
        def build(c, carry):
            named = (c // rb) * (groups * rb) + g * rb + lax.rem(c, rb)
            for b in range(hrows):
                at = jnp.int32(slots)
                for s in range(slots):
                    at = jnp.where(hc[b, 0, s] == named, s, at)
                hd[c, :, b * BS : (b + 1) * BS] = hst[b, at]
            return carry

        lax.fori_loop(0, nblk, build, 0)

    def tall(q, tile):
        return jnp.concatenate([tile] * (SIZES[q] // TILE), axis=0)

    def gone_of(q, who):
        return tall(q, bufs[0][CHUNKS - 1, who, full[-1] : full[-1] + TILE, :])

    def unpacked(gone, value):
        zero = jnp.zeros(gone.shape, BF16)
        out = []
        for c in range(cb):
            if c == 0:
                one = value(0)
            elif c == cb - 1:
                one = value(c - 1)
            else:
                one = jnp.where(gone < c, value(c - 1), value(c))
            out.append(jnp.where(gone == c, zero, one))
        return jnp.concatenate(out, axis=0)

    def operand(phase, who):
        step, q = divmod(phase, CHUNKS)
        if step == 0:
            return bufs[0][q, who, : full[q], :]
        return unpacked(gone_of(q, who), lambda p: bufs[step][q, who, part(q, p), :])

    def keep_apart(value, src, n):
        for b in range(rb):
            unp[(src * 2 + n) * rb + b, : value.shape[0]] = value[:, b * BS : (b + 1) * BS]

    def accumulate(phase, left, right, first):
        high = full[phase % CHUNKS]
        out = jnp.dot(left, right.reshape(left.shape[1], hrows * BS), preferred_element_type=F32)
        for k in range(groups):
            value = out[:, k * wide : (k + 1) * wide]
            acc[k, :high] = value if first else acc[k, :high] + value

    def multiply_half(phase, src, n):
        one = operand(phase, n * pairs + src)
        if dense:
            accumulate(phase, one, hd[pl.ds((src * 2 + n) * rb, rb)], False)
        else:
            keep_apart(one, src, n)

    def multiply(phase, src, first):
        both = [operand(phase, n * pairs + src) for n in range(2)]
        if dense:
            accumulate(phase, jnp.concatenate(both, axis=1), hd[pl.ds(src * 2 * rb, 2 * rb)], first)
        else:
            for n in range(2):
                keep_apart(both[n], src, n)

    def multiply_sparse(phase):
        high = full[phase % CHUNKS]

        def one_group(k, carry):
            for b in range(rb):
                i = k * rb + b
                out = jnp.zeros((high, BS), F32)
                for s in range(slots):
                    named = hc[i, 0, s]
                    at = named // (groups * rb) * rb + lax.rem(named, rb)
                    out = out + jnp.dot(unp[at][:high], hst[i, s], preferred_element_type=F32)
                acc[k, :high, b * BS : (b + 1) * BS] = out
            return carry

        lax.fori_loop(0, groups, one_group, 0)

    def forwarded(phase, src):
        got = piece(phase, (1 - core) * pairs + src)
        copy(got, got, ag_s.at[phase], fw_r.at[phase, src], row=sibling).wait_recv()

    def drain(phase):
        step, q = divmod(phase, CHUNKS)
        high = packed[q] if step else full[q] + (TILE if q == CHUNKS - 1 else 0)

        def settle(sem, counts):
            for n in sorted(set(counts) - {0}):

                def wait():
                    some = bufs[step].at[q, pl.ds(0, n), pl.ds(0, high)]
                    copy(some, some, sem.at[phase], sem.at[phase], row=sibling).wait_send()

                if len(set(counts)) == 1:
                    wait()
                else:
                    pl.when(pick(counts) == n)(wait)

        settle(ag_s, sent)
        settle(rl_s, passed)
        some = stage.at[phase, pl.ds(0, groups - 1), pl.ds(0, packed[q])]
        copy(some, some, rs_s.at[phase], rs_s.at[phase], row=sibling).wait_send()

    def pass_on(phase, n):
        src = order[n]
        got = piece(phase, core * pairs + src)
        copy(got, got, ag_s.at[phase], ag_r.at[phase, src], row=sibling).wait_recv()
        tos = [one[n] for one in onward]
        if any(to is not None for to in tos):
            to = pick([p if to is None else to for p, to in enumerate(tos)])
            go(
                copy(got, got, rl_s.at[phase], ag_r.at[phase, src], row=to * 2 + core),
                None if None not in tos else pick([int(one is not None) for one in tos]) == 1,
            )
        go(copy(got, got, ag_s.at[phase], fw_r.at[phase, src], row=sibling))

    def gather_multiply(phase):
        forwarded(phase, pair)
        multiply(phase, pair, True)
        last = len(order) - 1
        for n, src in enumerate(order):
            if n >= early - 1 and n < last:
                pass_on(phase, n + 1)
            if n < last:
                forwarded(phase, src)
                multiply(phase, src, False)
            else:
                multiply_half(phase, src, core)
                forwarded(phase, src)
                multiply_half(phase, src, 1 - core)
        if not dense:
            multiply_sparse(phase)

    def scatter_start(phase):
        q = phase % CHUNKS
        rows_here = pl.ds(0, packed[q])
        for k in [*range(groups - 1, 0, -1), 0]:
            to = partner(k)
            gone = tall(q, dgrp[to])
            for p in range(keeps):
                low, high = acc[to, part(q, p), :].astype(BF16), acc[to, part(q, p + 1), :].astype(BF16)
                stage[phase, to, part(q, p), :] = jnp.where(gone > p, low, high)
            if k:
                go(copy(stage.at[phase, to, rows_here], landed.at[phase, g, rows_here], rs_s.at[phase], rs_r.at[phase], grp=to))

    def scatter_finish(phase):
        step, q = divmod(phase, CHUNKS)
        got = landed.at[phase, pl.ds(0, groups - 1), pl.ds(0, packed[q])]
        copy(got, got, rs_s.at[phase], rs_r.at[phase], row=sibling).wait_recv()
        gone = tall(q, dgrp[g])
        for p in range(keeps):
            new = stage[phase, g, part(q, p), :].astype(F32)
            for k in range(1, groups):
                new = new + landed[phase, partner(k), part(q, p), :].astype(F32)
            if step == 1:
                old = jnp.where(gone > p, bufs[0][q, home, part(q, p), :], bufs[0][q, home, part(q, p + 1), :])
                new = 2.0 * new - old.astype(F32)
            elif step > 1:
                new = 2.0 * new - bufs[step - 1][q, home, part(q, p), :].astype(F32)
            if step < STEPS - 1:
                bufs[step + 1][q, home, part(q, p), :] = new.astype(BF16)
            else:
                stage[phase, g, part(q, p), :] = new.astype(BF16)
        if step < STEPS - 1:
            gather_start(phase + CHUNKS)

    def deliver(ref, source):
        pieces = [unpacked(tall(q, dgrp[g]), functools.partial(source, q)) for q in range(CHUNKS)]
        whole = jnp.concatenate([pieces[q][part(q, c), :] for c in range(cb) for q in range(CHUNKS)], axis=0)
        ref[...] = whole.T

    def first_part(phase):
        for n in range(early):
            pass_on(phase, n)

    turn_blocks()
    first_part(0)
    for q in range(AHEAD, CHUNKS):
        gather_start(q)
    if dense:
        lay_out()
    for phase in range(phases):
        gather_multiply(phase)
        if phase == 0:
            for k in range(1, groups):
                got = dgrp.at[partner(k)]
                copy(got, got, dg_s.at[k], dg_r.at[k], row=sibling).wait_recv()
        scatter_start(phase)
        if phase + 1 < phases:
            first_part(phase + 1)
        if phase:
            scatter_finish(phase - 1)
        if phase >= 3:
            drain(phase - 3)
    deliver(before_ref, lambda q, p: bufs[STEPS - 1][q, home, part(q, p), :])
    scatter_finish(phases - 1)
    deliver(last_ref, lambda q, p: stage[(STEPS - 1) * CHUNKS + q, g, part(q, p), :])
    for phase in range(phases - 3, phases):
        drain(phase)
    for k in range(1, groups):
        copy(dgrp.at[g], dgrp.at[g], dg_s.at[k], dg_r.at[k], row=sibling).wait_send()


def hand_out(before, last, before_hbm, last_hbm, sems):
    copies = [
        pltpu.make_async_copy(before, before_hbm, sems.at[0]),
        pltpu.make_async_copy(last, last_hbm, sems.at[1]),
    ]
    for one in copies:
        one.start()
    for one in copies:
        one.wait()


def per_device(t_start, h_blocks, h_cols, t_cols):
    groups, rows = lax.axis_size("grp"), lax.axis_size("row")
    rb, cb = t_start.shape[0] // BS, t_start.shape[1] // BS
    hrows, slots = h_blocks.shape[0], h_blocks.shape[2]
    keeps = t_cols.shape[1]
    nblk = rows * rb
    pairs = rows // 2
    wide = rb * BS
    dense = hrows * nblk * BS * BS * 2 <= DENSE_BYTES
    phases = STEPS * CHUNKS
    dma = pltpu.SemaphoreType.DMA
    out = pltpu.VMEM(t_start.shape, t_start.dtype)
    held = pl.pallas_call(
        functools.partial(kernel, (groups, rows, rb, cb, keeps, hrows, slots, dense)),
        out_shape=(out, out),
        in_specs=[
            pl.BlockSpec(memory_space=pl.ANY),
            pl.BlockSpec(memory_space=pl.ANY),
            pl.BlockSpec(memory_space=pl.ANY),
            pl.BlockSpec(memory_space=pl.ANY),
        ],
        out_specs=(pl.BlockSpec(memory_space=pltpu.VMEM),) * 2,
        scratch_shapes=[
            pltpu.VMEM((CHUNKS, rows, cb * WIDEST + TILE, wide), BF16),
            *[pltpu.VMEM((CHUNKS, rows, keeps * WIDEST, wide), BF16) for _ in range(STEPS - 1)],
            pltpu.VMEM(t_start.shape, BF16),
            pltpu.VMEM((hrows, slots, BS, BS), BF16),
            pltpu.VMEM((hrows, slots + 1, BS, BS), BF16),
            pltpu.VMEM((nblk, BS, hrows * BS) if dense else (1, TILE, BS), BF16),
            pltpu.VMEM((1, TILE, BS) if dense else (nblk, cb * WIDEST, BS), BF16),
            pltpu.VMEM((groups, cb * WIDEST, wide), F32),
            pltpu.VMEM((phases, groups, keeps * WIDEST, wide), BF16),
            pltpu.VMEM((phases, groups, keeps * WIDEST, wide), BF16),
            pltpu.VMEM((groups, TILE, wide), BF16),
            pltpu.SMEM(h_cols.shape, jnp.int32),
            pltpu.SMEM(t_cols.shape, jnp.int32),
            dma((phases,)),
            dma((phases,)),
            dma((phases,)),
            dma((phases,)),
            dma((phases, pairs)),
            dma((phases, pairs)),
            dma((groups,)),
            dma((groups,)),
            dma((4,)),
        ],
        compiler_params=pltpu.CompilerParams(
            collective_id=0, has_side_effects=True, vmem_limit_bytes=56 << 20
        ),
    )(t_start, h_blocks, h_cols, t_cols)
    out = jax.ShapeDtypeStruct(t_start.shape, t_start.dtype)
    return pl.pallas_call(
        hand_out,
        out_shape=(out, out),
        in_specs=[pl.BlockSpec(memory_space=pltpu.VMEM)] * 2,
        out_specs=(pl.BlockSpec(memory_space=pl.ANY),) * 2,
        scratch_shapes=[dma((2,))],
        name="hand_out",
    )(*[pltpu.with_memory_space_constraint(one, pltpu.VMEM) for one in held])


def solution(mesh):
    placed = (
        P(("row", "grp"), None),
        P("row", "grp", None, None, None),
        P("row", "grp", None),
        P(("row", "grp"), None),
    )
    return jax.shard_map(
        per_device,
        mesh=mesh,
        in_specs=placed,
        out_specs=(P(("row", "grp"), None), P(("row", "grp"), None)),
        check_vma=False,
    )
```
